32 devices in a mesh: pipe: 4 (over y, core), ctx: 4 (over z), tp: 2 (over x).
Axes of the slice: x: 2, y: 2, z: 4, core: 2. Of those that a mesh axis runs over, the one named last changes fastest.
Arguments:
- queries: bfloat16 [4, 512, 32, 128], P('pipe', 'ctx', 'tp'), may hold values from -45 to 45
- key_value: bfloat16 [4, 2, 512, 8, 128], P('pipe', None, 'ctx', 'tp'), may hold values from -6 to 6
- mamba_in: bfloat16 [4, 512, 8192], P('pipe', 'ctx', 'tp'), may hold values from -6 to 6
- gate_in: bfloat16 [4, 512, 8192], P('pipe', 'ctx', 'tp'), may hold values from -6 to 6
- step_low: bfloat16 [4, 512, 512], P('pipe', 'ctx'), may hold values from -3 to 3
- step_weight: bfloat16 [4, 512, 8192], P('pipe', None, 'tp'), may hold values from -0.25 to 0.25
- step_bias: float32 [4, 8192], P('pipe', 'tp'), may hold values from -4.6 to -3.2
- decay_rate: float32 [4, 8, 8192], P('pipe', None, 'tp'), may hold values from 0.048828125 to 2.5
- conv_weight: float32 [4, 4, 8192], P('pipe', None, 'tp'), may hold values from -3 to 3
- conv_bias: float32 [4, 8192], P('pipe', 'tp'), may hold values from -3 to 3
- state_weight: bfloat16 [4, 8192, 16], P('pipe', 'tp'), may hold values from -0.0625 to 0.0625
- skip_gain: float32 [4, 8192], P('pipe', 'tp'), may hold values from 0.5 to 1.5
Outputs:
- attended: bfloat16 [4, 512, 32, 128], P('pipe', 'ctx', 'tp')
- mamba_out: bfloat16 [4, 512, 8192], P('pipe', 'ctx', 'tp')
The draws below stay inside these ranges and needn't reach their ends.
All inputs are finite; a program needn't handle non-finite values.
Results may differ from the reference program's by a relative error of at most 0.023.
Values may be sent and summed in bfloat16 or wider, within the bound.
A program may use at most 64 MiB of HBM per device.

```python
import math
import jax
import jax.numpy as jnp
from jax import lax

Q_HEADS = 32
KV_HEADS = 8
HEAD_DIM = 128
INNER = 8192
STATE = 8
STEP_RANK = 512
CONV = 4
SEQ = 512
SECTIONS = 4


def attention_inputs(key):
    key_part = jax.random.fold_in(key, 11)
    value_part = jax.random.fold_in(key, 12)
    query_part = jax.random.fold_in(key, 13)
    key_shape = (SECTIONS, SEQ, KV_HEADS, HEAD_DIM)
    query_shape = (SECTIONS, SEQ, Q_HEADS, HEAD_DIM)
    keys = jax.random.truncated_normal(key_part, -6.0, 6.0, key_shape, jnp.float32)
    values = jax.random.truncated_normal(value_part, -6.0, 6.0, key_shape, jnp.float32)
    queries = jax.random.truncated_normal(query_part, -6.0, 6.0, query_shape, jnp.float32)
    return (queries, jnp.stack([keys, values], axis=1))


def draw_queries(key, part):
    return attention_inputs(key)[0].astype(jnp.bfloat16)


def draw_key_value(key, part):
    return attention_inputs(key)[1].astype(jnp.bfloat16)


def draw_decay_rate(key, part):
    kind_key = jax.random.fold_in(key, 21)
    fast_key = jax.random.fold_in(key, 22)
    slow_key = jax.random.fold_in(key, 23)
    shape = (SECTIONS, STATE, INNER)
    fast_channel = jax.random.bernoulli(kind_key, 0.5, (SECTIONS, 1, INNER))
    slow_rate = jnp.exp(jax.random.uniform(slow_key, shape, jnp.float32, math.log(0.5), math.log(2.0))) / (0.02 * SEQ)
    fast_rate = jnp.exp(jax.random.uniform(fast_key, shape, jnp.float32, math.log(0.8), math.log(2.5)))
    return jnp.where(fast_channel, fast_rate, slow_rate)


def levels(stream_key, shape, pieces, low, top_value):
    gain = 1.0
    for axis_at, shards_of in pieces:
        heights = jax.random.uniform(jax.random.fold_in(jax.random.fold_in(stream_key, 6), axis_at), (shards_of,), jnp.float32, low / len(pieces), top_value / len(pieces))
        gain = gain * jnp.repeat(jnp.exp(heights), shape[axis_at] // shards_of).reshape((-1,) + (1,) * (len(shape) - 1 - axis_at))
    return gain


def bell_draw(own_key, dims, width, limit, pieces=(), held_as=jnp.bfloat16):
    values = jax.random.normal(own_key, dims, jnp.float32) * width
    if len(pieces) > 0:
        values = levels(own_key, dims, pieces, -0.22, 0.18) * values
    return jnp.clip(values, min=-limit, max=limit).astype(held_as)


def setup_inputs(seed: int = 0) -> dict:
    seeds = jax.random.split(jax.random.key(seed), 13)
    return {
        "queries": draw_queries(jax.random.fold_in(seeds[12], 71), 0),
        "key_value": draw_key_value(jax.random.fold_in(seeds[12], 71), 0),
        "mamba_in": bell_draw(seeds[2], (SECTIONS, SEQ, INNER), 1.0, 6.0, ((0, 4), (1, 4), (2, 2))),
        "gate_in": bell_draw(seeds[3], (SECTIONS, SEQ, INNER), 1.0, 6.0, ((0, 4), (1, 4), (2, 2))),
        "step_low": bell_draw(seeds[4], (SECTIONS, SEQ, STEP_RANK), 0.5, 3.0, ((0, 4), (1, 4))),
        "step_weight": bell_draw(seeds[5], (SECTIONS, STEP_RANK, INNER), STEP_RANK ** -0.5, 0.25, ((0, 4), (2, 2))),
        "step_bias": jnp.clip(-4.6 + 1.3999999 * jax.random.uniform(seeds[6], (SECTIONS, INNER), jnp.float32) ** levels(seeds[6], (SECTIONS, INNER), ((0, 4), (1, 2)), -0.2, 0.2), -4.6, -3.2),
        "decay_rate": draw_decay_rate(jax.random.fold_in(seeds[12], 71), 0),
        "conv_weight": bell_draw(seeds[8], (SECTIONS, CONV, INNER), 0.5, 3.0, ((0, 4), (2, 2)), jnp.float32),
        "conv_bias": bell_draw(seeds[9], (SECTIONS, INNER), 0.5, 3.0, ((0, 4), (1, 2)), jnp.float32),
        "state_weight": bell_draw(seeds[10], (SECTIONS, INNER, 2 * STATE), INNER ** -0.5, 0.0625, ((0, 4), (1, 2))),
        "skip_gain": jnp.clip(0.5 + 1.0 * jax.random.uniform(seeds[11], (SECTIONS, INNER), jnp.float32) ** levels(seeds[11], (SECTIONS, INNER), ((0, 4), (1, 2)), -0.2, 0.2), 0.5, 1.5),
    }


def attention_section(queries, key_value):
    group_size = Q_HEADS // KV_HEADS
    positions = jnp.arange(SEQ, dtype=jnp.int32)
    causal = positions[:, None] >= positions[None, :]

    def single_head(head):
        query_head = queries[:, head, :]
        key_head = key_value[0, :, head // group_size, :]
        value_head = key_value[1, :, head // group_size, :]
        scores = jnp.dot(query_head, key_head.T, preferred_element_type=jnp.float32) / math.sqrt(HEAD_DIM)
        scores = jnp.where(causal, scores, -jnp.inf)
        maximum = lax.optimization_barrier(jnp.max(scores, axis=1, keepdims=True))
        expterm = jnp.exp(scores - maximum)
        denominator = lax.optimization_barrier(jnp.sum(expterm, axis=1, keepdims=True))
        mixed = jnp.dot(expterm.astype(jnp.bfloat16), value_head, preferred_element_type=jnp.float32) / denominator
        return mixed.astype(jnp.bfloat16)
    heads_out = lax.map(single_head, jnp.arange(Q_HEADS, dtype=jnp.int32))
    return jnp.transpose(heads_out, (1, 0, 2))

def mamba_section(mamba_in, gate_in, step_low, step_weight, step_bias, decay_rate, conv_weight, conv_bias, state_weight, skip_gain):
    padded = jnp.concatenate([jnp.zeros((CONV - 1, INNER), jnp.float32), mamba_in.astype(jnp.float32)], axis=0)
    conv_out = conv_bias[None, :]
    for tap_index in range(CONV):
        conv_out = conv_out + conv_weight[tap_index][None, :] * padded[tap_index:tap_index + SEQ]
    inner_act = jax.nn.silu(conv_out).astype(jnp.bfloat16)
    entry_read = jnp.dot(inner_act, state_weight, preferred_element_type=jnp.float32)
    entry_map = entry_read[:, :STATE]
    read_map = entry_read[:, STATE:]
    step_size = jax.nn.softplus(jnp.dot(step_low, step_weight, preferred_element_type=jnp.float32) + step_bias[None, :])
    drive_input = step_size * inner_act.astype(jnp.float32)

    def advance(carry_state, row_data):
        step_row, drive_row, entry_row, read_row = row_data
        carry_state = jnp.exp(-decay_rate * step_row[None, :]) * carry_state + entry_row[:, None] * drive_row[None, :]
        return (carry_state, lax.optimization_barrier(jnp.sum(read_row[:, None] * carry_state, axis=0)))
    _, scanned = lax.scan(advance, jnp.zeros((STATE, INNER), jnp.float32), (step_size, drive_input, entry_map, read_map))
    scan_out = scanned + skip_gain[None, :] * inner_act.astype(jnp.float32)
    return (scan_out * jax.nn.silu(gate_in.astype(jnp.float32))).astype(jnp.bfloat16)

def attention_pair(pair):
    return attention_section(pair[0], pair[1])

def mamba_group(group):
    return mamba_section(*group)

def reference(queries, key_value, mamba_in, gate_in, step_low, step_weight, step_bias, decay_rate, conv_weight, conv_bias, state_weight, skip_gain):
    mixed = lax.map(attention_pair, (queries, key_value))
    gated = lax.map(mamba_group, (mamba_in, gate_in, step_low, step_weight, step_bias, decay_rate, conv_weight, conv_bias, state_weight, skip_gain))
    return (jnp.roll(mixed, 1, axis=0), jnp.roll(gated, 1, axis=0))
```

```python
import functools
import math

import jax
import jax.numpy as jnp
from jax import lax
from jax.experimental import pallas as pl
from jax.experimental.pallas import tpu as pltpu
from jax.sharding import PartitionSpec as P

F32 = jnp.float32
BF16 = jnp.bfloat16
MESH = pl.DeviceIdType.MESH
CHUNK = 32
HALO = 16


def nt_dot(a, b, precision=None):
    return lax.dot_general(
        a, b, (((1,), (1,)), ((), ())), precision=precision, preferred_element_type=F32
    )


def silu(v):
    return v / (1.0 + jnp.exp(-v))


def kernel(
    sizes,
    q_hbm,
    kv_hbm,
    x_hbm,
    gate_hbm,
    low_hbm,
    sw_hbm,
    bias_ref,
    decay_ref,
    cw_ref,
    cb_ref,
    ew_ref,
    skip_ref,
    att_out,
    mam_out,
    q_v,
    kv_v,
    x_v,
    gate_v,
    low_v,
    sw_v,
    kv_all,
    halo,
    pad_v,
    act_v,
    step_v,
    drive_v,
    y_v,
    h_v,
    ebc_v,
    rb_v,
    part_v,
    tp_in,
    hend_v,
    ent_v,
    dtot_v,
    chain_out,
    chain_in,
    att_stage,
    mam_stage,
    local_sem,
    halo_sem,
    kv_send,
    kv_recv,
    tp_send,
    tp_recv,
    chain_sem,
    att_sem,
    mam_send,
    mam_recv,
):
    nctx, ntp, npipe = sizes
    T, C = x_v.shape
    heads, _, D = q_v.shape
    kvh = kv_v.shape[0] // 2
    group = heads // kvh
    N = decay_ref.shape[0]
    taps = cw_ref.shape[0]
    W = h_v.shape[1]
    G = C // W
    B = pad_v.shape[1]

    me = lax.axis_index("ctx")
    tp = lax.axis_index("tp")
    pipe = lax.axis_index("pipe")
    nxt = lax.rem(pipe + 1, npipe)
    prv = lax.rem(pipe + npipe - 1, npipe)

    local = []
    for i, (src, dst) in enumerate(
        (
            (x_hbm, x_v),
            (low_hbm, low_v),
            (sw_hbm, sw_v),
            (kv_hbm, kv_v),
            (q_hbm, q_v),
            (gate_hbm, gate_v),
        )
    ):
        copy = pltpu.make_async_copy(src, dst, local_sem.at[i])
        copy.start()
        local.append(copy)
    x_copy, low_copy, sw_copy, kv_copy, q_copy, gate_copy = local

    barrier = pltpu.get_barrier_semaphore()
    for d in range(1, nctx):
        pl.semaphore_signal(
            barrier, inc=1, device_id={"ctx": lax.rem(me + d, nctx)}, device_id_type=MESH
        )
    for d in range(1, ntp):
        pl.semaphore_signal(
            barrier, inc=1, device_id={"tp": lax.rem(tp + d, ntp)}, device_id_type=MESH
        )
    pl.semaphore_signal(barrier, inc=1, device_id={"pipe": nxt}, device_id_type=MESH)
    pl.semaphore_signal(barrier, inc=1, device_id={"pipe": prv}, device_id_type=MESH)
    pl.semaphore_wait(barrier, nctx - 1 + ntp - 1 + 2)

    later = jnp.minimum(me + 1, nctx - 1)
    halo_copy = pltpu.make_async_remote_copy(
        src_ref=x_hbm.at[pl.ds(T - HALO, HALO)],
        dst_ref=halo,
        send_sem=halo_sem.at[0],
        recv_sem=halo_sem.at[1],
        device_id={"ctx": later},
        device_id_type=MESH,
    )

    @pl.when(me + 1 < nctx)
    def _():
        halo_copy.start()

    def kv_copy_to(d):
        return pltpu.make_async_remote_copy(
            src_ref=kv_hbm,
            dst_ref=kv_all.at[me],
            send_sem=kv_send.at[d - 1],
            recv_sem=kv_recv.at[me],
            device_id={"ctx": jnp.minimum(me + d, nctx - 1)},
            device_id_type=MESH,
        )

    for d in range(1, nctx):

        @pl.when(me + d < nctx)
        def _(d=d):
            kv_copy_to(d).start()

    x_copy.wait()

    @pl.when(me > 0)
    def _():
        halo_copy.wait_recv()

    @pl.when(me == 0)
    def _():
        halo[...] = jnp.zeros_like(halo)

    part_v[...] = jnp.zeros_like(part_v)

    @pl.loop(0, C // B)
    def _(b):
        lanes = pl.ds(pl.multiple_of(b * B, B), B)
        pad_v[0:HALO, :] = halo[:, lanes].astype(F32)
        pad_v[HALO:, :] = x_v[:, lanes].astype(F32)
        conv = cb_ref[:, lanes]
        for k in range(taps):
            conv = conv + cw_ref[k : k + 1, lanes] * pad_v[pl.ds(HALO - (taps - 1) + k, T), :]
        act = silu(conv).astype(BF16)
        act_v[:, lanes] = act
        part_v[...] += nt_dot(ew_ref[:, lanes], act)

    def tp_copy(d):
        return pltpu.make_async_remote_copy(
            src_ref=part_v,
            dst_ref=tp_in.at[tp],
            send_sem=tp_send.at[d - 1],
            recv_sem=tp_recv.at[tp],
            device_id={"tp": lax.rem(tp + d, ntp)},
            device_id_type=MESH,
        )

    for d in range(1, ntp):
        tp_copy(d).start()

    low_copy.wait()
    sw_copy.wait()

    @pl.loop(0, C // B)
    def _(b):
        lanes = pl.ds(pl.multiple_of(b * B, B), B)
        v = jnp.dot(low_v[...], sw_v[:, lanes], preferred_element_type=F32) + bias_ref[:, lanes]
        step = jnp.maximum(v, 0.0) + jnp.log1p(jnp.exp(-jnp.abs(v)))
        step_v[:, lanes] = step
        drive_v[:, lanes] = step * act_v[:, lanes].astype(F32)
        dtot_v[:, lanes] = jnp.exp(
            -decay_ref[:, lanes] * jnp.sum(step, axis=0, keepdims=True)
        )

    entry = part_v[...]
    for d in range(1, ntp):
        other = lax.rem(tp + d, ntp)
        pltpu.make_async_remote_copy(
            src_ref=part_v,
            dst_ref=tp_in.at[other],
            send_sem=tp_send.at[d - 1],
            recv_sem=tp_recv.at[other],
            device_id={"tp": other},
            device_id_type=MESH,
        ).wait_recv()
        entry = entry + tp_in[other]

    for t in range(T):
        ebc_v[t * N : (t + 1) * N, :] = jnp.broadcast_to(entry[:N, t : t + 1], (N, 128))
    hi = lax.Precision.HIGHEST
    rows = lax.broadcasted_iota(jnp.int32, (T, T), 0)
    cols = lax.broadcasted_iota(jnp.int32, (T, T), 1)
    by_pos = nt_dot((rows == cols).astype(F32), entry, hi)
    width = CHUNK * N
    srow = lax.broadcasted_iota(jnp.int32, (2 * N, width), 0)
    scol = lax.broadcasted_iota(jnp.int32, (2 * N, width), 1)
    pick = (srow == N + lax.rem(scol, N)).astype(F32)
    spread = jnp.dot(by_pos, pick, precision=hi, preferred_element_type=F32)
    mrow = lax.rem(lax.broadcasted_iota(jnp.int32, (T, width), 0), CHUNK)
    mcol = lax.div(lax.broadcasted_iota(jnp.int32, (T, width), 1), N)
    rb_v[...] = jnp.where(mrow == mcol, spread, 0.0).astype(BF16)

    def run(lanes, start, driven):
        rate = -decay_ref[:, lanes]

        def pair(i, h):
            both = []
            for k in range(8):
                t = i * 8 + k
                decay = jnp.exp(rate * step_v[pl.ds(t, 1), lanes])
                h = decay * h
                if driven:
                    e = ebc_v[pl.ds(pl.multiple_of(t * N, N), N), :]
                    h = h + jnp.concatenate([e] * (W // 128), axis=1) * drive_v[pl.ds(t, 1), lanes]
                both.append(h)
                if k % 2 == 1:
                    h_v[pl.ds(pl.multiple_of((t - 1) * N, 2 * N), 2 * N), :] = jnp.concatenate(
                        both, axis=0
                    ).astype(BF16)
                    both = []
            return h

        return lax.fori_loop(0, T // 8, pair, start)

    def read_out(k):
        return jnp.dot(
            rb_v[k * CHUNK : (k + 1) * CHUNK, :],
            h_v[k * width : (k + 1) * width, :],
            preferred_element_type=F32,
        )

    @pl.loop(0, G)
    def _(g):
        lanes = pl.ds(pl.multiple_of(g * W, W), W)
        hend_v[:, lanes] = run(lanes, jnp.zeros((N, W), F32), True)
        for k in range(T // CHUNK):
            part = slice(k * CHUNK, (k + 1) * CHUNK)
            y_v[part, lanes] = read_out(k) + skip_ref[:, lanes] * act_v[part, lanes].astype(F32)

    half = C // 2
    chain_copy = pltpu.make_async_remote_copy(
        src_ref=chain_out,
        dst_ref=chain_in,
        send_sem=chain_sem.at[0],
        recv_sem=chain_sem.at[1],
        device_id={"ctx": later},
        device_id_type=MESH,
    )

    @pl.when(me > 0)
    def _():
        chain_copy.wait_recv()
        for s in range(2):
            cols = slice(s * half, (s + 1) * half)
            ent_v[:, cols] = chain_in[...].astype(F32)[s * N : (s + 1) * N, :]

    @pl.when(me == 0)
    def _():
        ent_v[...] = jnp.zeros_like(ent_v)

    @pl.when(me + 1 < nctx)
    def _():
        out = dtot_v[...] * ent_v[...] + hend_v[...]
        chain_out[...] = jnp.concatenate([out[:, :half], out[:, half:]], axis=0).astype(BF16)
        chain_copy.start()

    kv_copy.wait()
    q_copy.wait()

    def kv_wait(j, carry):
        pltpu.make_async_remote_copy(
            src_ref=kv_hbm,
            dst_ref=kv_all.at[j],
            send_sem=kv_send.at[0],
            recv_sem=kv_recv.at[j],
            device_id={"ctx": later},
            device_id_type=MESH,
        ).wait_recv()
        return carry

    lax.fori_loop(0, me, kv_wait, 0)
    scale = 1.0 / math.sqrt(D)
    qrow = lax.rem(lax.broadcasted_iota(jnp.int32, (group * T, T), 0), T)
    kcol = lax.broadcasted_iota(jnp.int32, (group * T, T), 1)
    seen = kcol <= qrow
    for g in range(kvh):
        q = q_v[g * group : (g + 1) * group].reshape(group * T, D)
        s = jnp.where(seen, nt_dot(q, kv_v[g]) * scale, -1e30)
        top = jnp.max(s, axis=1, keepdims=True)
        p = jnp.exp(s - top)
        total = jnp.sum(p, axis=1, keepdims=True)
        acc = jnp.dot(p.astype(BF16), kv_v[kvh + g], preferred_element_type=F32)

        def block(j, carry, q=q, g=g):
            top, total, acc = carry
            s = nt_dot(q, kv_all[j, g]) * scale
            new = jnp.maximum(top, jnp.max(s, axis=1, keepdims=True))
            fade = jnp.exp(top - new)
            p = jnp.exp(s - new)
            total = total * fade + jnp.sum(p, axis=1, keepdims=True)
            acc = acc * fade + jnp.dot(
                p.astype(BF16), kv_all[j, kvh + g], preferred_element_type=F32
            )
            return new, total, acc

        top, total, acc = lax.fori_loop(0, me, block, (top, total, acc))
        att_stage[g * group : (g + 1) * group] = (acc / total).astype(BF16).reshape(group, T, D)

    att_copy = pltpu.make_async_remote_copy(
        src_ref=att_stage,
        dst_ref=att_out,
        send_sem=att_sem.at[0],
        recv_sem=att_sem.at[1],
        device_id={"pipe": nxt},
        device_id_type=MESH,
    )
    att_copy.start()

    gate_copy.wait()

    def mam_copy(g):
        lanes = pl.ds(pl.multiple_of(g * W, W), W)
        return pltpu.make_async_remote_copy(
            src_ref=mam_stage.at[:, lanes],
            dst_ref=mam_out.at[:, lanes],
            send_sem=mam_send.at[g],
            recv_sem=mam_recv.at[g],
            device_id={"pipe": nxt},
            device_id_type=MESH,
        )

    @pl.loop(0, G)
    def _(g):
        lanes = pl.ds(pl.multiple_of(g * W, W), W)

        @pl.when(me > 0)
        def _():
            run(lanes, ent_v[:, lanes], False)
            for k in range(T // CHUNK):
                part = slice(k * CHUNK, (k + 1) * CHUNK)
                y_v[part, lanes] += read_out(k)

        for k in range(T // CHUNK):
            part = slice(k * CHUNK, (k + 1) * CHUNK)
            gate = gate_v[part, lanes].astype(F32)
            mam_stage[part, lanes] = (y_v[part, lanes] * silu(gate)).astype(BF16)
        mam_copy(g).start()

    @pl.when(me + 1 < nctx)
    def _():
        halo_copy.wait_send()
        chain_copy.wait_send()

    for d in range(1, nctx):

        @pl.when(me + d < nctx)
        def _(d=d):
            kv_copy_to(d).wait_send()

    for d in range(1, ntp):
        tp_copy(d).wait_send()
    att_copy.wait()

    @pl.loop(0, G)
    def _(g):
        mam_copy(g).wait()


def per_device(
    sizes,
    queries,
    key_value,
    mamba_in,
    gate_in,
    step_low,
    step_weight,
    step_bias,
    decay_rate,
    conv_weight,
    conv_bias,
    state_weight,
    skip_gain,
):
    nctx, ntp, _ = sizes
    T, H, D = queries.shape[1:]
    kvh = key_value.shape[3]
    C = mamba_in.shape[2]
    R = step_low.shape[2]
    N = decay_rate.shape[1]
    W = min(1024, C // 2)
    B = 256
    q = jnp.transpose(queries[0], (1, 0, 2))
    kv = jnp.transpose(key_value[0], (0, 2, 1, 3)).reshape(2 * kvh, T, D)
    anywhere = pl.BlockSpec(memory_space=pl.ANY)
    vmem = pl.BlockSpec(memory_space=pltpu.VMEM)
    dma = pltpu.SemaphoreType.DMA
    att, mam = pl.pallas_call(
        functools.partial(kernel, sizes),
        out_shape=(
            jax.ShapeDtypeStruct((H, T, D), BF16),
            jax.ShapeDtypeStruct((T, C), BF16),
        ),
        in_specs=[anywhere] * 6 + [vmem] * 6,
        out_specs=(anywhere, anywhere),
        scratch_shapes=[
            pltpu.VMEM((H, T, D), BF16),
            pltpu.VMEM((2 * kvh, T, D), BF16),
            pltpu.VMEM((T, C), BF16),
            pltpu.VMEM((T, C), BF16),
            pltpu.VMEM((T, R), BF16),
            pltpu.VMEM((R, C), BF16),
            pltpu.VMEM((nctx, 2 * kvh, T, D), BF16),
            pltpu.VMEM((HALO, C), BF16),
            pltpu.VMEM((HALO + T, B), F32),
            pltpu.VMEM((T, C), BF16),
            pltpu.VMEM((T, C), F32),
            pltpu.VMEM((T, C), F32),
            pltpu.VMEM((T, C), F32),
            pltpu.VMEM((T * N, W), BF16),
            pltpu.VMEM((T * N, 128), F32),
            pltpu.VMEM((T, CHUNK * N), BF16),
            pltpu.VMEM((2 * N, T), F32),
            pltpu.VMEM((ntp, 2 * N, T), F32),
            pltpu.VMEM((N, C), F32),
            pltpu.VMEM((N, C), F32),
            pltpu.VMEM((N, C), F32),
            pltpu.VMEM((2 * N, C // 2), BF16),
            pltpu.VMEM((2 * N, C // 2), BF16),
            pltpu.VMEM((H, T, D), BF16),
            pltpu.VMEM((T, C), BF16),
            dma((6,)),
            dma((2,)),
            dma((max(1, nctx - 1),)),
            dma((nctx,)),
            dma((max(1, ntp - 1),)),
            dma((ntp,)),
            dma((2,)),
            dma((2,)),
            dma((C // W,)),
            dma((C // W,)),
        ],
        compiler_params=pltpu.CompilerParams(
            collective_id=0, has_side_effects=True, vmem_limit_bytes=50 * 2**20
        ),
    )(
        q,
        kv,
        mamba_in[0],
        gate_in[0],
        step_low[0],
        step_weight[0],
        step_bias,
        decay_rate[0],
        conv_weight[0],
        conv_bias,
        state_weight[0].T,
        skip_gain,
    )
    return jnp.transpose(att, (1, 0, 2))[None], mam[None]


def solution(mesh):
    sizes = (mesh.shape["ctx"], mesh.shape["tp"], mesh.shape["pipe"])
    return jax.shard_map(
        functools.partial(per_device, sizes),
        mesh=mesh,
        in_specs=(
            P("pipe", "ctx", "tp", None),
            P("pipe", None, "ctx", "tp", None),
            P("pipe", "ctx", "tp"),
            P("pipe", "ctx", "tp"),
            P("pipe", "ctx", None),
            P("pipe", None, "tp"),
            P("pipe", "tp"),
            P("pipe", None, "tp"),
            P("pipe", None, "tp"),
            P("pipe", "tp"),
            P("pipe", "tp", None),
            P("pipe", "tp"),
        ),
        out_specs=(P("pipe", "ctx", "tp", None), P("pipe", "ctx", "tp")),
        check_vma=False,
    )
```

```python
import functools
import math

import jax
import jax.numpy as jnp
from jax import lax
from jax.experimental import pallas as pl
from jax.experimental.pallas import tpu as pltpu
from jax.sharding import PartitionSpec as P

F32 = jnp.float32
BF16 = jnp.bfloat16
MESH = pl.DeviceIdType.MESH
CHUNK = 32
HALO = 16


def nt_dot(a, b, precision=None):
    return lax.dot_general(
        a, b, (((1,), (1,)), ((), ())), precision=precision, preferred_element_type=F32
    )


def silu(v):
    return 0.5 * v * (1.0 + jnp.tanh(0.5 * v))


def kernel(
    sizes,
    q_hbm,
    kv_hbm,
    x_hbm,
    gate_hbm,
    low_hbm,
    sw_hbm,
    bias_hbm,
    decay_hbm,
    cw_hbm,
    cb_hbm,
    ew_hbm,
    skip_hbm,
    att_out,
    mam_out,
    q_v,
    kv_v,
    x_v,
    gate_v,
    low_v,
    sw_v,
    bias_ref,
    decay_ref,
    cw_ref,
    cb_ref,
    ew_ref,
    skip_ref,
    kv_all,
    halo,
    pad_v,
    act_v,
    step_v,
    drive_v,
    y_v,
    h_v,
    ebc_v,
    rb_v,
    part_v,
    tp_in,
    hend_v,
    ent_v,
    dtot_v,
    chain_out,
    chain_in,
    att_stage,
    mam_stage,
    local_sem,
    halo_sem,
    kv_send,
    kv_recv,
    tp_send,
    tp_recv,
    chain_send,
    chain_recv,
    att_sem,
    over_send,
    over_recv,
    mam_send,
    mam_recv,
):
    nctx, ntp, npipe = sizes
    T, C = x_v.shape
    heads, _, D = q_v.shape
    kvh = kv_v.shape[0] // 2
    group = heads // kvh
    N = decay_ref.shape[0]
    taps = cw_ref.shape[0]
    W = h_v.shape[1]
    G = C // W
    B = pad_v.shape[1]

    me = lax.axis_index("ctx")
    tp = lax.axis_index("tp")
    pipe = lax.axis_index("pipe")
    nxt = lax.rem(pipe + 1, npipe)
    prv = lax.rem(pipe + npipe - 1, npipe)

    local = []
    for i, (src, dst) in enumerate(
        (
            (x_hbm, x_v),
            (cw_hbm, cw_ref),
            (cb_hbm, cb_ref),
            (ew_hbm, ew_ref),
            (low_hbm, low_v),
            (sw_hbm, sw_v),
            (bias_hbm, bias_ref),
            (decay_hbm, decay_ref),
            (skip_hbm, skip_ref),
            (gate_hbm, gate_v),
        )
    ):
        copy = pltpu.make_async_copy(src, dst, local_sem.at[i])
        copy.start()
        local.append(copy)

    barrier = pltpu.get_barrier_semaphore()
    for d in range(1, nctx):
        pl.semaphore_signal(
            barrier, inc=1, device_id={"ctx": lax.rem(me + d, nctx)}, device_id_type=MESH
        )
    for d in range(1, ntp):
        pl.semaphore_signal(
            barrier, inc=1, device_id={"tp": lax.rem(tp + d, ntp)}, device_id_type=MESH
        )
    pl.semaphore_signal(barrier, inc=1, device_id={"pipe": nxt}, device_id_type=MESH)
    pl.semaphore_signal(barrier, inc=1, device_id={"pipe": prv}, device_id_type=MESH)
    pl.semaphore_wait(barrier, nctx - 1 + ntp - 1 + 2)

    later = jnp.minimum(me + 1, nctx - 1)
    halo_copy = pltpu.make_async_remote_copy(
        src_ref=x_hbm.at[pl.ds(T - HALO, HALO)],
        dst_ref=halo,
        send_sem=halo_sem.at[0],
        recv_sem=halo_sem.at[1],
        device_id={"ctx": later},
        device_id_type=MESH,
    )

    @pl.when(me + 1 < nctx)
    def _():
        halo_copy.start()

    over = []
    for i, (src, dst) in enumerate(((kv_hbm, kv_v), (q_hbm, q_v))):
        copy = pltpu.make_async_remote_copy(
            src_ref=src,
            dst_ref=dst,
            send_sem=over_send.at[i],
            recv_sem=over_recv.at[i],
            device_id={"pipe": nxt},
            device_id_type=MESH,
        )
        copy.start()
        over.append(copy)

    for copy in local[:4]:
        copy.wait()

    @pl.when(me > 0)
    def _():
        halo_copy.wait_recv()

    @pl.when(me == 0)
    def _():
        halo[...] = jnp.zeros_like(halo)

    part_v[...] = jnp.zeros_like(part_v)

    @pl.loop(0, C // B)
    def _(b):
        lanes = pl.ds(pl.multiple_of(b * B, B), B)
        pad_v[0:HALO, :] = halo[:, lanes].astype(F32)
        pad_v[HALO:, :] = x_v[:, lanes].astype(F32)
        conv = cb_ref[:, lanes]
        for k in range(taps):
            conv = conv + cw_ref[k : k + 1, lanes] * pad_v[pl.ds(HALO - (taps - 1) + k, T), :]
        act = silu(conv).astype(BF16)
        act_v[:, lanes] = act
        part_v[...] += nt_dot(ew_ref[:, lanes], act)

    def tp_copy(d):
        return pltpu.make_async_remote_copy(
            src_ref=part_v,
            dst_ref=tp_in.at[tp],
            send_sem=tp_send.at[d - 1],
            recv_sem=tp_recv.at[tp],
            device_id={"tp": lax.rem(tp + d, ntp)},
            device_id_type=MESH,
        )

    for d in range(1, ntp):
        tp_copy(d).start()

    over[0].wait_recv()

    def kv_copy_to(d):
        return pltpu.make_async_remote_copy(
            src_ref=kv_v,
            dst_ref=kv_all.at[me],
            send_sem=kv_send.at[d - 1],
            recv_sem=kv_recv.at[me],
            device_id={"ctx": jnp.minimum(me + d, nctx - 1)},
            device_id_type=MESH,
        )

    for d in range(1, nctx):

        @pl.when(me + d < nctx)
        def _(d=d):
            kv_copy_to(d).start()

    for copy in local[4:9]:
        copy.wait()

    @pl.loop(0, C // B)
    def _(b):
        lanes = pl.ds(pl.multiple_of(b * B, B), B)
        v = jnp.dot(low_v[...], sw_v[:, lanes], preferred_element_type=F32) + bias_ref[:, lanes]
        step = jnp.maximum(v, 0.0) + jnp.log1p(jnp.exp(-jnp.abs(v)))
        step_v[:, lanes] = step
        drive_v[:, lanes] = step * act_v[:, lanes].astype(F32)
        dtot_v[:, lanes] = jnp.exp(
            -decay_ref[:, lanes] * jnp.sum(step, axis=0, keepdims=True)
        )

    entry = part_v[...]
    for d in range(1, ntp):
        other = lax.rem(tp + d, ntp)
        pltpu.make_async_remote_copy(
            src_ref=part_v,
            dst_ref=tp_in.at[other],
            send_sem=tp_send.at[d - 1],
            recv_sem=tp_recv.at[other],
            device_id={"tp": other},
            device_id_type=MESH,
        ).wait_recv()
        entry = entry + tp_in[other]

    for t in range(T):
        ebc_v[t * N : (t + 1) * N, :] = jnp.broadcast_to(entry[:N, t : t + 1], (N, 128))
    hi = lax.Precision.HIGHEST
    rows = lax.broadcasted_iota(jnp.int32, (T, T), 0)
    cols = lax.broadcasted_iota(jnp.int32, (T, T), 1)
    by_pos = nt_dot((rows == cols).astype(F32), entry, hi)
    width = CHUNK * N
    srow = lax.broadcasted_iota(jnp.int32, (2 * N, width), 0)
    scol = lax.broadcasted_iota(jnp.int32, (2 * N, width), 1)
    pick = (srow == N + lax.rem(scol, N)).astype(F32)
    spread = jnp.dot(by_pos, pick, precision=hi, preferred_element_type=F32)
    mrow = lax.rem(lax.broadcasted_iota(jnp.int32, (T, width), 0), CHUNK)
    mcol = lax.div(lax.broadcasted_iota(jnp.int32, (T, width), 1), N)
    rb_v[...] = jnp.where(mrow == mcol, spread, 0.0).astype(BF16)

    def run(lanes, start, driven):
        rate = -decay_ref[:, lanes]

        def pair(i, h):
            both = []
            for k in range(16):
                t = i * 16 + k
                decay = jnp.exp(rate * step_v[pl.ds(t, 1), lanes])
                h = decay * h
                if driven:
                    e = ebc_v[pl.ds(pl.multiple_of(t * N, N), N), :]
                    h = h + jnp.concatenate([e] * (W // 128), axis=1) * drive_v[pl.ds(t, 1), lanes]
                both.append(h)
                if k % 2 == 1:
                    h_v[pl.ds(pl.multiple_of((t - 1) * N, 2 * N), 2 * N), :] = jnp.concatenate(
                        both, axis=0
                    ).astype(BF16)
                    both = []
            return h

        return lax.fori_loop(0, T // 16, pair, start)

    def read_out(k):
        return jnp.dot(
            rb_v[k * CHUNK : (k + 1) * CHUNK, :],
            h_v[k * width : (k + 1) * width, :],
            preferred_element_type=F32,
        )

    half = W // 2

    def chain_copy(g):
        return pltpu.make_async_remote_copy(
            src_ref=chain_out.at[g],
            dst_ref=chain_in.at[g],
            send_sem=chain_send.at[g],
            recv_sem=chain_recv.at[g],
            device_id={"ctx": later},
            device_id_type=MESH,
        )

    def hand_down(g):
        lanes = pl.ds(pl.multiple_of(g * W, W), W)

        @pl.when(me == 0)
        def _():
            ent_v[:, lanes] = jnp.zeros((N, W), F32)

        @pl.when(me > 0)
        def _():
            chain_copy(g).wait_recv()
            both = chain_in[g].astype(F32)
            ent_v[:, lanes] = jnp.concatenate([both[:N], both[N:]], axis=1)

        @pl.when(me + 1 < nctx)
        def _():
            out = dtot_v[:, lanes] * ent_v[:, lanes] + hend_v[:, lanes]
            chain_out[g] = jnp.concatenate([out[:, :half], out[:, half:]], axis=0).astype(BF16)
            chain_copy(g).start()

    @pl.loop(0, G)
    def _(g):
        lanes = pl.ds(pl.multiple_of(g * W, W), W)
        hend_v[:, lanes] = run(lanes, jnp.zeros((N, W), F32), True)
        for k in range(T // CHUNK):
            part = slice(k * CHUNK, (k + 1) * CHUNK)
            y_v[part, lanes] = read_out(k) + skip_ref[:, lanes] * act_v[part, lanes].astype(F32)

        @pl.when(g >= me)
        def _():
            hand_down(g - me)

    local[9].wait()

    def mam_copy(g):
        lanes = pl.ds(pl.multiple_of(g * W, W), W)
        return pltpu.make_async_remote_copy(
            src_ref=mam_stage.at[:, lanes],
            dst_ref=mam_out.at[:, lanes],
            send_sem=mam_send.at[g],
            recv_sem=mam_recv.at[g],
            device_id={"pipe": nxt},
            device_id_type=MESH,
        )

    def finish(g):
        lanes = pl.ds(pl.multiple_of(g * W, W), W)

        @pl.when(me > 0)
        def _():
            run(lanes, ent_v[:, lanes], False)
            for k in range(T // CHUNK):
                part = slice(k * CHUNK, (k + 1) * CHUNK)
                y_v[part, lanes] += read_out(k)

        for k in range(T // CHUNK):
            part = slice(k * CHUNK, (k + 1) * CHUNK)
            gate = gate_v[part, lanes].astype(F32)
            mam_stage[part, lanes] = (y_v[part, lanes] * silu(gate)).astype(BF16)
        mam_copy(g).start()

    lag = max(0, nctx - 1 - G)

    @pl.loop(0, lag + G)
    def _(i):
        @pl.when((G + i >= me) & (i < me))
        def _():
            hand_down(G + i - me)

        @pl.when(i >= lag)
        def _():
            finish(i - lag)

    over[1].wait_recv()

    def kv_wait(j, carry):
        pltpu.make_async_remote_copy(
            src_ref=kv_v,
            dst_ref=kv_all.at[j],
            send_sem=kv_send.at[0],
            recv_sem=kv_recv.at[j],
            device_id={"ctx": later},
            device_id_type=MESH,
        ).wait_recv()
        return carry

    lax.fori_loop(0, me, kv_wait, 0)
    scale = 1.0 / math.sqrt(D)
    qrow = lax.rem(lax.broadcasted_iota(jnp.int32, (group * T, T), 0), T)
    kcol = lax.broadcasted_iota(jnp.int32, (group * T, T), 1)
    seen = kcol <= qrow
    for g in range(kvh):
        q = q_v[g * group : (g + 1) * group].reshape(group * T, D)
        s = jnp.where(seen, nt_dot(q, kv_v[g]) * scale, -1e30)
        top = jnp.max(s, axis=1, keepdims=True)
        p = jnp.exp(s - top)
        total = jnp.sum(p, axis=1, keepdims=True)
        acc = jnp.dot(p.astype(BF16), kv_v[kvh + g], preferred_element_type=F32)

        def block(j, carry, q=q, g=g):
            top, total, acc = carry
            s = nt_dot(q, kv_all[j, g]) * scale
            new = jnp.maximum(top, jnp.max(s, axis=1, keepdims=True))
            fade = jnp.exp(top - new)
            p = jnp.exp(s - new)
            total = total * fade + jnp.sum(p, axis=1, keepdims=True)
            acc = acc * fade + jnp.dot(
                p.astype(BF16), kv_all[j, kvh + g], preferred_element_type=F32
            )
            return new, total, acc

        top, total, acc = lax.fori_loop(0, me, block, (top, total, acc))
        att_stage[g * group : (g + 1) * group] = (acc / total).astype(BF16).reshape(group, T, D)

    att_copy = pltpu.make_async_copy(att_stage, att_out, att_sem)
    att_copy.start()

    @pl.when(me + 1 < nctx)
    def _():
        halo_copy.wait_send()

        @pl.loop(0, G)
        def _(g):
            chain_copy(g).wait_send()

    for d in range(1, nctx):

        @pl.when(me + d < nctx)
        def _(d=d):
            kv_copy_to(d).wait_send()

    for d in range(1, ntp):
        tp_copy(d).wait_send()
    for copy in over:
        copy.wait_send()
    att_copy.wait()

    @pl.loop(0, G)
    def _(g):
        mam_copy(g).wait()


def per_device(
    sizes,
    queries,
    key_value,
    mamba_in,
    gate_in,
    step_low,
    step_weight,
    step_bias,
    decay_rate,
    conv_weight,
    conv_bias,
    state_weight,
    skip_gain,
):
    nctx, ntp, _ = sizes
    T, H, D = queries.shape[1:]
    kvh = key_value.shape[3]
    C = mamba_in.shape[2]
    R = step_low.shape[2]
    N = decay_rate.shape[1]
    W = min(1024, C // 2)
    B = 256
    q = jnp.transpose(queries[0], (1, 0, 2))
    kv = jnp.transpose(key_value[0], (0, 2, 1, 3)).reshape(2 * kvh, T, D)
    anywhere = pl.BlockSpec(memory_space=pl.ANY)
    dma = pltpu.SemaphoreType.DMA
    att, mam = pl.pallas_call(
        functools.partial(kernel, sizes),
        out_shape=(
            jax.ShapeDtypeStruct((H, T, D), BF16),
            jax.ShapeDtypeStruct((T, C), BF16),
        ),
        in_specs=[anywhere] * 12,
        out_specs=(anywhere, anywhere),
        scratch_shapes=[
            pltpu.VMEM((H, T, D), BF16),
            pltpu.VMEM((2 * kvh, T, D), BF16),
            pltpu.VMEM((T, C), BF16),
            pltpu.VMEM((T, C), BF16),
            pltpu.VMEM((T, R), BF16),
            pltpu.VMEM((R, C), BF16),
            pltpu.VMEM((1, C), F32),
            pltpu.VMEM((N, C), F32),
            pltpu.VMEM(conv_weight.shape[1:], F32),
            pltpu.VMEM((1, C), F32),
            pltpu.VMEM((2 * N, C), BF16),
            pltpu.VMEM((1, C), F32),
            pltpu.VMEM((nctx, 2 * kvh, T, D), BF16),
            pltpu.VMEM((HALO, C), BF16),
            pltpu.VMEM((HALO + T, B), F32),
            pltpu.VMEM((T, C), BF16),
            pltpu.VMEM((T, C), F32),
            pltpu.VMEM((T, C), F32),
            pltpu.VMEM((T, C), F32),
            pltpu.VMEM((T * N, W), BF16),
            pltpu.VMEM((T * N, 128), F32),
            pltpu.VMEM((T, CHUNK * N), BF16),
            pltpu.VMEM((2 * N, T), F32),
            pltpu.VMEM((ntp, 2 * N, T), F32),
            pltpu.VMEM((N, C), F32),
            pltpu.VMEM((N, C), F32),
            pltpu.VMEM((N, C), F32),
            pltpu.VMEM((C // W, 2 * N, W // 2), BF16),
            pltpu.VMEM((C // W, 2 * N, W // 2), BF16),
            pltpu.VMEM((H, T, D), BF16),
            pltpu.VMEM((T, C), BF16),
            dma((10,)),
            dma((2,)),
            dma((max(1, nctx - 1),)),
            dma((nctx,)),
            dma((max(1, ntp - 1),)),
            dma((ntp,)),
            dma((C // W,)),
            dma((C // W,)),
            dma,
            dma((2,)),
            dma((2,)),
            dma((C // W,)),
            dma((C // W,)),
        ],
        compiler_params=pltpu.CompilerParams(
            collective_id=0, has_side_effects=True, vmem_limit_bytes=60 * 2**20
        ),
    )(
        q,
        kv,
        mamba_in[0],
        gate_in[0],
        step_low[0],
        step_weight[0],
        step_bias,
        decay_rate[0],
        conv_weight[0],
        conv_bias,
        state_weight[0].T,
        skip_gain,
    )
    return jnp.transpose(att, (1, 0, 2))[None], mam[None]


def solution(mesh):
    sizes = (mesh.shape["ctx"], mesh.shape["tp"], mesh.shape["pipe"])
    return jax.shard_map(
        functools.partial(per_device, sizes),
        mesh=mesh,
        in_specs=(
            P("pipe", "ctx", "tp", None),
            P("pipe", None, "ctx", "tp", None),
            P("pipe", "ctx", "tp"),
            P("pipe", "ctx", "tp"),
            P("pipe", "ctx", None),
            P("pipe", None, "tp"),
            P("pipe", "tp"),
            P("pipe", None, "tp"),
            P("pipe", None, "tp"),
            P("pipe", "tp"),
            P("pipe", "tp", None),
            P("pipe", "tp"),
        ),
        out_specs=(P("pipe", "ctx", "tp", None), P("pipe", "ctx", "tp")),
        check_vma=False,
    )
```

```python
import functools
import math

import jax
import jax.numpy as jnp
from jax import lax
from jax.experimental import pallas as pl
from jax.experimental.pallas import tpu as pltpu
from jax.sharding import PartitionSpec as P

F32 = jnp.float32
BF16 = jnp.bfloat16
MESH = pl.DeviceIdType.MESH
CHUNK = 32
HALO = 16


def nt_dot(a, b, precision=None):
    return lax.dot_general(
        a, b, (((1,), (1,)), ((), ())), precision=precision, preferred_element_type=F32
    )


def silu(v):
    return 0.5 * v * (1.0 + jnp.tanh(0.5 * v))


def kernel(
    sizes,
    q_hbm,
    kv_hbm,
    x_hbm,
    gate_hbm,
    low_hbm,
    sw_hbm,
    bias_hbm,
    decay_hbm,
    cw_hbm,
    cb_hbm,
    ew_hbm,
    skip_hbm,
    att_out,
    mam_out,
    q_v,
    score_v,
    top_v,
    x_v,
    gate_v,
    low_v,
    sw_v,
    bias_ref,
    decay_ref,
    cw_ref,
    cb_ref,
    ew_ref,
    skip_ref,
    kv_all,
    halo,
    pad_v,
    act_v,
    step_v,
    drive_v,
    y_v,
    h_v,
    ebc_v,
    rb_v,
    part_v,
    tp_in,
    hend_v,
    ent_v,
    dtot_v,
    chain_out,
    chain_in,
    att_stage,
    mam_stage,
    local_sem,
    halo_sem,
    kv_send,
    kv_recv,
    tp_send,
    tp_recv,
    chain_send,
    chain_recv,
    att_sem,
    over_send,
    over_recv,
    mam_send,
    mam_recv,
):
    nctx, ntp, npipe = sizes
    T, C = x_v.shape
    heads, _, D = q_v.shape
    kvh = kv_all.shape[1] // 2
    group = heads // kvh
    N = decay_ref.shape[0]
    taps = cw_ref.shape[0]
    W = h_v.shape[1]
    G = C // W
    B = pad_v.shape[1]

    me = lax.axis_index("ctx")
    tp = lax.axis_index("tp")
    pipe = lax.axis_index("pipe")
    nxt = lax.rem(pipe + 1, npipe)
    prv = lax.rem(pipe + npipe - 1, npipe)

    local = []
    for i, (src, dst) in enumerate(
        (
            (x_hbm, x_v),
            (cw_hbm, cw_ref),
            (cb_hbm, cb_ref),
            (ew_hbm, ew_ref),
            (low_hbm, low_v),
            (sw_hbm, sw_v),
            (bias_hbm, bias_ref),
            (decay_hbm, decay_ref),
            (skip_hbm, skip_ref),
            (gate_hbm, gate_v),
        )
    ):
        copy = pltpu.make_async_copy(src, dst, local_sem.at[i])
        copy.start()
        local.append(copy)

    barrier = pltpu.get_barrier_semaphore()
    for d in range(1, nctx):
        pl.semaphore_signal(
            barrier, inc=1, device_id={"ctx": lax.rem(me + d, nctx)}, device_id_type=MESH
        )
    for d in range(1, ntp):
        pl.semaphore_signal(
            barrier, inc=1, device_id={"tp": lax.rem(tp + d, ntp)}, device_id_type=MESH
        )
    pl.semaphore_signal(barrier, inc=1, device_id={"pipe": nxt}, device_id_type=MESH)
    pl.semaphore_signal(barrier, inc=1, device_id={"pipe": prv}, device_id_type=MESH)
    pl.semaphore_wait(barrier, nctx - 1 + ntp - 1 + 2)

    later = jnp.minimum(me + 1, nctx - 1)
    halo_copy = pltpu.make_async_remote_copy(
        src_ref=x_hbm.at[pl.ds(T - HALO, HALO)],
        dst_ref=halo,
        send_sem=halo_sem.at[0],
        recv_sem=halo_sem.at[1],
        device_id={"ctx": later},
        device_id_type=MESH,
    )

    @pl.when(me + 1 < nctx)
    def _():
        halo_copy.start()

    over = []
    for i, (src, dst) in enumerate(((kv_hbm, kv_all.at[me]), (q_hbm, q_v))):
        copy = pltpu.make_async_remote_copy(
            src_ref=src,
            dst_ref=dst,
            send_sem=over_send.at[i],
            recv_sem=over_recv.at[i],
            device_id={"pipe": nxt},
            device_id_type=MESH,
        )
        copy.start()
        over.append(copy)

    def kv_copy(r):
        j = jnp.maximum(me - r, 0)
        return pltpu.make_async_remote_copy(
            src_ref=kv_all.at[j],
            dst_ref=kv_all.at[j],
            send_sem=kv_send.at[r],
            recv_sem=kv_recv.at[j],
            device_id={"ctx": later},
            device_id_type=MESH,
        )

    def kv_pass(r):
        kv_copy(r).wait_recv()

        @pl.when(me + 1 < nctx)
        def _():
            kv_copy(r).start()

    for copy in local[:4]:
        copy.wait()

    @pl.when(me > 0)
    def _():
        halo_copy.wait_recv()

    @pl.when(me == 0)
    def _():
        halo[...] = jnp.zeros_like(halo)

    over[0].wait_recv()

    @pl.when(me + 1 < nctx)
    def _():
        kv_copy(0).start()

    part_v[...] = jnp.zeros_like(part_v)

    @pl.loop(0, C // B)
    def _(b):
        lanes = pl.ds(pl.multiple_of(b * B, B), B)
        pad_v[0:HALO, :] = halo[:, lanes].astype(F32)
        pad_v[HALO:, :] = x_v[:, lanes].astype(F32)
        conv = cb_ref[:, lanes]
        for k in range(taps):
            conv = conv + cw_ref[k : k + 1, lanes] * pad_v[pl.ds(HALO - (taps - 1) + k, T), :]
        act = silu(conv).astype(BF16)
        act_v[:, lanes] = act
        part_v[...] += nt_dot(ew_ref[:, lanes], act)

    def tp_copy(d):
        return pltpu.make_async_remote_copy(
            src_ref=part_v,
            dst_ref=tp_in.at[tp],
            send_sem=tp_send.at[d - 1],
            recv_sem=tp_recv.at[tp],
            device_id={"tp": lax.rem(tp + d, ntp)},
            device_id_type=MESH,
        )

    for d in range(1, ntp):
        tp_copy(d).start()

    for copy in local[4:9]:
        copy.wait()

    @pl.loop(0, C // B)
    def _(b):
        lanes = pl.ds(pl.multiple_of(b * B, B), B)
        v = jnp.dot(low_v[...], sw_v[:, lanes], preferred_element_type=F32) + bias_ref[:, lanes]
        step = jnp.maximum(v, 0.0) + jnp.log1p(jnp.exp(-jnp.abs(v)))
        step_v[:, lanes] = step
        drive_v[:, lanes] = step * act_v[:, lanes].astype(F32)
        dtot_v[:, lanes] = jnp.exp(
            -decay_ref[:, lanes] * jnp.sum(step, axis=0, keepdims=True)
        )

    @pl.when((me >= 1) & (me + 1 < nctx))
    def _():
        kv_pass(1)

    entry = part_v[...]
    for d in range(1, ntp):
        other = lax.rem(tp + d, ntp)
        pltpu.make_async_remote_copy(
            src_ref=part_v,
            dst_ref=tp_in.at[other],
            send_sem=tp_send.at[d - 1],
            recv_sem=tp_recv.at[other],
            device_id={"tp": other},
            device_id_type=MESH,
        ).wait_recv()
        entry = entry + tp_in[other]

    for t in range(T):
        ebc_v[t * N : (t + 1) * N, :] = jnp.broadcast_to(entry[:N, t : t + 1], (N, 128))
    hi = lax.Precision.HIGHEST
    rows = lax.broadcasted_iota(jnp.int32, (T, T), 0)
    cols = lax.broadcasted_iota(jnp.int32, (T, T), 1)
    by_pos = nt_dot((rows == cols).astype(F32), entry, hi)
    width = CHUNK * N
    srow = lax.broadcasted_iota(jnp.int32, (2 * N, width), 0)
    scol = lax.broadcasted_iota(jnp.int32, (2 * N, width), 1)
    pick = (srow == N + lax.rem(scol, N)).astype(F32)
    spread = jnp.dot(by_pos, pick, precision=hi, preferred_element_type=F32)
    mrow = lax.rem(lax.broadcasted_iota(jnp.int32, (T, width), 0), CHUNK)
    mcol = lax.div(lax.broadcasted_iota(jnp.int32, (T, width), 1), N)
    rb_v[...] = jnp.where(mrow == mcol, spread, 0.0).astype(BF16)

    def run(lanes, start, driven):
        rate = -decay_ref[:, lanes]

        def pair(i, h):
            both = []
            for k in range(16):
                t = i * 16 + k
                decay = jnp.exp(rate * step_v[pl.ds(t, 1), lanes])
                h = decay * h
                if driven:
                    e = ebc_v[pl.ds(pl.multiple_of(t * N, N), N), :]
                    h = h + jnp.concatenate([e] * (W // 128), axis=1) * drive_v[pl.ds(t, 1), lanes]
                both.append(h)
                if k % 2 == 1:
                    h_v[pl.ds(pl.multiple_of((t - 1) * N, 2 * N), 2 * N), :] = jnp.concatenate(
                        both, axis=0
                    ).astype(BF16)
                    both = []
            return h

        return lax.fori_loop(0, T // 16, pair, start)

    def read_out(k):
        return jnp.dot(
            rb_v[k * CHUNK : (k + 1) * CHUNK, :],
            h_v[k * width : (k + 1) * width, :],
            preferred_element_type=F32,
        )

    half = W // 2

    def chain_copy(g):
        return pltpu.make_async_remote_copy(
            src_ref=chain_out.at[g],
            dst_ref=chain_in.at[g],
            send_sem=chain_send.at[g],
            recv_sem=chain_recv.at[g],
            device_id={"ctx": later},
            device_id_type=MESH,
        )

    def hand_down(g):
        lanes = pl.ds(pl.multiple_of(g * W, W), W)

        @pl.when(me == 0)
        def _():
            ent_v[:, lanes] = jnp.zeros((N, W), F32)

        @pl.when(me > 0)
        def _():
            chain_copy(g).wait_recv()
            both = chain_in[g].astype(F32)
            ent_v[:, lanes] = jnp.concatenate([both[:N], both[N:]], axis=1)

        @pl.when(me + 1 < nctx)
        def _():
            out = dtot_v[:, lanes] * ent_v[:, lanes] + hend_v[:, lanes]
            chain_out[g] = jnp.concatenate([out[:, :half], out[:, half:]], axis=0).astype(BF16)
            chain_copy(g).start()

    @pl.loop(0, G)
    def _(g):
        lanes = pl.ds(pl.multiple_of(g * W, W), W)
        hend_v[:, lanes] = run(lanes, jnp.zeros((N, W), F32), True)
        for k in range(T // CHUNK):
            part = slice(k * CHUNK, (k + 1) * CHUNK)
            y_v[part, lanes] = read_out(k) + skip_ref[:, lanes] * act_v[part, lanes].astype(F32)

        @pl.when(g >= me)
        def _():
            hand_down(g - me)

        @pl.when((g >= 1) & (g + 1 <= me) & (me + 1 < nctx))
        def _():
            kv_pass(g + 1)

    local[9].wait()

    def mam_copy(g):
        lanes = pl.ds(pl.multiple_of(g * W, W), W)
        return pltpu.make_async_remote_copy(
            src_ref=mam_stage.at[:, lanes],
            dst_ref=mam_out.at[:, lanes],
            send_sem=mam_send.at[g],
            recv_sem=mam_recv.at[g],
            device_id={"pipe": nxt},
            device_id_type=MESH,
        )

    def finish(g):
        lanes = pl.ds(pl.multiple_of(g * W, W), W)

        @pl.when(me > 0)
        def _():
            run(lanes, ent_v[:, lanes], False)
            for k in range(T // CHUNK):
                part = slice(k * CHUNK, (k + 1) * CHUNK)
                y_v[part, lanes] += read_out(k)

        for k in range(T // CHUNK):
            part = slice(k * CHUNK, (k + 1) * CHUNK)
            gate = gate_v[part, lanes].astype(F32)
            mam_stage[part, lanes] = (y_v[part, lanes] * silu(gate)).astype(BF16)
        mam_copy(g).start()

    lag = max(0, nctx - 1 - G)

    @pl.loop(0, lag + G)
    def _(i):
        @pl.when((G + i >= me) & (i < me))
        def _():
            hand_down(G + i - me)

        @pl.when(i >= lag)
        def _():
            finish(i - lag)

    over[1].wait_recv()

    @pl.loop(jnp.where(me + 1 < nctx, G + 1, 1), me + 1)
    def _(r):
        kv_pass(r)

    scale = 1.0 / math.sqrt(D)
    rows_of = lax.broadcasted_iota(jnp.int32, (group * T, T), 0)
    seen = lax.broadcasted_iota(jnp.int32, (group * T, T), 1) <= lax.rem(rows_of, T)
    ones = jnp.ones((T, 128), BF16)

    def query(g):
        return q_v[g * group : (g + 1) * group].reshape(group * T, D)

    for g in range(kvh):
        s = jnp.where(seen, nt_dot(query(g), kv_all[me, g]), -1e30)
        score_v[g, me] = s
        top_v[g] = s

    @pl.loop(0, me)
    def _(j):
        for g in range(kvh):
            s = nt_dot(query(g), kv_all[j, g])
            score_v[g, j] = s
            top_v[g] = jnp.maximum(top_v[g], s)

    for g in range(kvh):
        top_v[g] = jnp.broadcast_to(jnp.max(top_v[g], axis=1, keepdims=True), (group * T, T))

    def weigh(g, j):
        p = jnp.exp((score_v[g, j] - top_v[g]) * scale).astype(BF16)
        values = jnp.concatenate([kv_all[j, kvh + g], ones], axis=1)
        return jnp.dot(p, values, preferred_element_type=F32)

    for g in range(kvh):
        acc = lax.fori_loop(0, me, lambda j, acc, g=g: acc + weigh(g, j), weigh(g, me))
        out = (acc[:, :D] / acc[:, D:]).astype(BF16)
        att_stage[g * group : (g + 1) * group] = out.reshape(group, T, D)

    att_copy = pltpu.make_async_copy(att_stage, att_out, att_sem)
    att_copy.start()

    @pl.when(me + 1 < nctx)
    def _():
        halo_copy.wait_send()

        @pl.loop(0, G)
        def _(g):
            chain_copy(g).wait_send()

    @pl.when(me + 1 < nctx)
    def _():
        @pl.loop(0, me + 1)
        def _(r):
            kv_copy(r).wait_send()

    for d in range(1, ntp):
        tp_copy(d).wait_send()
    for copy in over:
        copy.wait_send()
    att_copy.wait()

    @pl.loop(0, G)
    def _(g):
        mam_copy(g).wait()


def per_device(
    sizes,
    queries,
    key_value,
    mamba_in,
    gate_in,
    step_low,
    step_weight,
    step_bias,
    decay_rate,
    conv_weight,
    conv_bias,
    state_weight,
    skip_gain,
):
    nctx, ntp, _ = sizes
    T, H, D = queries.shape[1:]
    kvh = key_value.shape[3]
    C = mamba_in.shape[2]
    R = step_low.shape[2]
    N = decay_rate.shape[1]
    W = min(1024, C // 2)
    B = 256
    q = jnp.transpose(queries[0], (1, 0, 2))
    kv = jnp.transpose(key_value[0], (0, 2, 1, 3)).reshape(2 * kvh, T, D)
    anywhere = pl.BlockSpec(memory_space=pl.ANY)
    dma = pltpu.SemaphoreType.DMA
    att, mam = pl.pallas_call(
        functools.partial(kernel, sizes),
        out_shape=(
            jax.ShapeDtypeStruct((H, T, D), BF16),
            jax.ShapeDtypeStruct((T, C), BF16),
        ),
        in_specs=[anywhere] * 12,
        out_specs=(anywhere, anywhere),
        scratch_shapes=[
            pltpu.VMEM((H, T, D), BF16),
            pltpu.VMEM((kvh, nctx, H // kvh * T, T), F32),
            pltpu.VMEM((kvh, H // kvh * T, T), F32),
            pltpu.VMEM((T, C), BF16),
            pltpu.VMEM((T, C), BF16),
            pltpu.VMEM((T, R), BF16),
            pltpu.VMEM((R, C), BF16),
            pltpu.VMEM((1, C), F32),
            pltpu.VMEM((N, C), F32),
            pltpu.VMEM(conv_weight.shape[1:], F32),
            pltpu.VMEM((1, C), F32),
            pltpu.VMEM((2 * N, C), BF16),
            pltpu.VMEM((1, C), F32),
            pltpu.VMEM((nctx, 2 * kvh, T, D), BF16),
            pltpu.VMEM((HALO, C), BF16),
            pltpu.VMEM((HALO + T, B), F32),
            pltpu.VMEM((T, C), BF16),
            pltpu.VMEM((T, C), F32),
            pltpu.VMEM((T, C), F32),
            pltpu.VMEM((T, C), F32),
            pltpu.VMEM((T * N, W), BF16),
            pltpu.VMEM((T * N, 128), F32),
            pltpu.VMEM((T, CHUNK * N), BF16),
            pltpu.VMEM((2 * N, T), F32),
            pltpu.VMEM((ntp, 2 * N, T), F32),
            pltpu.VMEM((N, C), F32),
            pltpu.VMEM((N, C), F32),
            pltpu.VMEM((N, C), F32),
            pltpu.VMEM((C // W, 2 * N, W // 2), BF16),
            pltpu.VMEM((C // W, 2 * N, W // 2), BF16),
            pltpu.VMEM((H, T, D), BF16),
            pltpu.VMEM((T, C), BF16),
            dma((10,)),
            dma((2,)),
            dma((nctx,)),
            dma((nctx,)),
            dma((max(1, ntp - 1),)),
            dma((ntp,)),
            dma((C // W,)),
            dma((C // W,)),
            dma,
            dma((2,)),
            dma((2,)),
            dma((C // W,)),
            dma((C // W,)),
        ],
        compiler_params=pltpu.CompilerParams(
            collective_id=0, has_side_effects=True, vmem_limit_bytes=60 * 2**20
        ),
    )(
        q,
        kv,
        mamba_in[0],
        gate_in[0],
        step_low[0],
        step_weight[0],
        step_bias,
        decay_rate[0],
        conv_weight[0],
        conv_bias,
        state_weight[0].T,
        skip_gain,
    )
    return jnp.transpose(att, (1, 0, 2))[None], mam[None]


def solution(mesh):
    sizes = (mesh.shape["ctx"], mesh.shape["tp"], mesh.shape["pipe"])
    return jax.shard_map(
        functools.partial(per_device, sizes),
        mesh=mesh,
        in_specs=(
            P("pipe", "ctx", "tp", None),
            P("pipe", None, "ctx", "tp", None),
            P("pipe", "ctx", "tp"),
            P("pipe", "ctx", "tp"),
            P("pipe", "ctx", None),
            P("pipe", None, "tp"),
            P("pipe", "tp"),
            P("pipe", None, "tp"),
            P("pipe", None, "tp"),
            P("pipe", "tp"),
            P("pipe", "tp", None),
            P("pipe", "tp"),
        ),
        out_specs=(P("pipe", "ctx", "tp", None), P("pipe", "ctx", "tp")),
        check_vma=False,
    )
```

```python
import functools
import math

import jax
import jax.numpy as jnp
from jax import lax
from jax.experimental import pallas as pl
from jax.experimental.pallas import tpu as pltpu
from jax.sharding import PartitionSpec as P

F32 = jnp.float32
BF16 = jnp.bfloat16
MESH = pl.DeviceIdType.MESH
CHUNK = 32
HALO = 16
UNROLL = 16


def nt_dot(a, b, precision=None):
    return lax.dot_general(
        a, b, (((1,), (1,)), ((), ())), precision=precision, preferred_element_type=F32
    )


def silu(v):
    return 0.5 * v * (1.0 + jnp.tanh(0.5 * v))


def kernel(
    sizes,
    q_hbm,
    kv_hbm,
    x_hbm,
    gate_hbm,
    low_hbm,
    sw_hbm,
    bias_hbm,
    decay_hbm,
    cw_hbm,
    cb_hbm,
    ew_hbm,
    skip_hbm,
    att_out,
    mam_out,
    q_v,
    score_v,
    top_v,
    x_v,
    gate_v,
    low_v,
    sw_v,
    bias_ref,
    decay_ref,
    cw_ref,
    cb_ref,
    ew_ref,
    skip_ref,
    kv_all,
    halo,
    pad_v,
    act_v,
    step_v,
    drive_v,
    y_v,
    h_v,
    ebc_v,
    rb_v,
    part_v,
    tp_in,
    hend_v,
    ent_v,
    dtot_v,
    chain_out,
    chain_in,
    att_stage,
    mam_stage,
    local_sem,
    halo_sem,
    kv_send,
    kv_recv,
    tp_send,
    tp_recv,
    chain_send,
    chain_recv,
    att_sem,
    over_send,
    over_recv,
    mam_send,
    mam_recv,
):
    nctx, ntp, npipe = sizes
    T, C = x_v.shape
    heads, _, D = q_v.shape
    kvh = kv_all.shape[1] // 2
    group = heads // kvh
    N = decay_ref.shape[0]
    taps = cw_ref.shape[0]
    W = h_v.shape[1]
    G = C // W
    B = pad_v.shape[1]

    me = lax.axis_index("ctx")
    tp = lax.axis_index("tp")
    pipe = lax.axis_index("pipe")
    nxt = lax.rem(pipe + 1, npipe)
    prv = lax.rem(pipe + npipe - 1, npipe)

    local = []
    for i, (src, dst) in enumerate(
        (
            (x_hbm, x_v),
            (cw_hbm, cw_ref),
            (cb_hbm, cb_ref),
            (ew_hbm, ew_ref),
            (low_hbm, low_v),
            (sw_hbm, sw_v),
            (bias_hbm, bias_ref),
            (decay_hbm, decay_ref),
            (skip_hbm, skip_ref),
            (gate_hbm, gate_v),
        )
    ):
        copy = pltpu.make_async_copy(src, dst, local_sem.at[i])
        copy.start()
        local.append(copy)

    barrier = pltpu.get_barrier_semaphore()
    for d in range(1, nctx):
        pl.semaphore_signal(
            barrier, inc=1, device_id={"ctx": lax.rem(me + d, nctx)}, device_id_type=MESH
        )
    for d in range(1, ntp):
        pl.semaphore_signal(
            barrier, inc=1, device_id={"tp": lax.rem(tp + d, ntp)}, device_id_type=MESH
        )
    pl.semaphore_signal(barrier, inc=1, device_id={"pipe": nxt}, device_id_type=MESH)
    pl.semaphore_signal(barrier, inc=1, device_id={"pipe": prv}, device_id_type=MESH)
    pl.semaphore_wait(barrier, nctx - 1 + ntp - 1 + 2)

    later = jnp.minimum(me + 1, nctx - 1)
    halo_copy = pltpu.make_async_remote_copy(
        src_ref=x_hbm.at[pl.ds(T - HALO, HALO)],
        dst_ref=halo,
        send_sem=halo_sem.at[0],
        recv_sem=halo_sem.at[1],
        device_id={"ctx": later},
        device_id_type=MESH,
    )

    @pl.when(me + 1 < nctx)
    def _():
        halo_copy.start()

    over = []
    for i, (src, dst) in enumerate(((kv_hbm, kv_all.at[me]), (q_hbm, q_v))):
        copy = pltpu.make_async_remote_copy(
            src_ref=src,
            dst_ref=dst,
            send_sem=over_send.at[i],
            recv_sem=over_recv.at[i],
            device_id={"pipe": nxt},
            device_id_type=MESH,
        )
        copy.start()
        over.append(copy)

    def kv_copy(r):
        j = jnp.maximum(me - r, 0)
        return pltpu.make_async_remote_copy(
            src_ref=kv_all.at[j],
            dst_ref=kv_all.at[j],
            send_sem=kv_send.at[r],
            recv_sem=kv_recv.at[j],
            device_id={"ctx": later},
            device_id_type=MESH,
        )

    def kv_pass(r):
        kv_copy(r).wait_recv()

        @pl.when(me + 1 < nctx)
        def _():
            kv_copy(r).start()

    for copy in local[:4]:
        copy.wait()

    @pl.when(me > 0)
    def _():
        halo_copy.wait_recv()

    @pl.when(me == 0)
    def _():
        halo[...] = jnp.zeros_like(halo)

    over[0].wait_recv()

    @pl.when(me + 1 < nctx)
    def _():
        kv_copy(0).start()

    part_v[...] = jnp.zeros_like(part_v)

    @pl.loop(0, C // B)
    def _(b):
        lanes = pl.ds(pl.multiple_of(b * B, B), B)
        pad_v[0:HALO, :] = halo[:, lanes].astype(F32)
        pad_v[HALO:, :] = x_v[:, lanes].astype(F32)
        conv = cb_ref[:, lanes]
        for k in range(taps):
            conv = conv + cw_ref[k : k + 1, lanes] * pad_v[pl.ds(HALO - (taps - 1) + k, T), :]
        act = silu(conv).astype(BF16)
        act_v[:, lanes] = act
        part_v[...] += nt_dot(ew_ref[:, lanes], act)

    def tp_copy(d):
        return pltpu.make_async_remote_copy(
            src_ref=part_v,
            dst_ref=tp_in.at[tp],
            send_sem=tp_send.at[d - 1],
            recv_sem=tp_recv.at[tp],
            device_id={"tp": lax.rem(tp + d, ntp)},
            device_id_type=MESH,
        )

    for d in range(1, ntp):
        tp_copy(d).start()

    for copy in local[4:9]:
        copy.wait()

    @pl.loop(0, C // B)
    def _(b):
        lanes = pl.ds(pl.multiple_of(b * B, B), B)
        v = jnp.dot(low_v[...], sw_v[:, lanes], preferred_element_type=F32) + bias_ref[:, lanes]
        step = jnp.maximum(v, 0.0) + jnp.log1p(jnp.exp(-jnp.abs(v)))
        drive = step * act_v[:, lanes].astype(F32)
        for i in range(B // 128):
            cols = slice(i * 128, (i + 1) * 128)
            step_v[b * (B // 128) + i] = step[:, cols]
            drive_v[b * (B // 128) + i] = drive[:, cols]
        dtot_v[:, lanes] = jnp.exp(
            -decay_ref[:, lanes] * jnp.sum(step, axis=0, keepdims=True)
        )

    @pl.when((me >= 1) & (me + 1 < nctx))
    def _():
        kv_pass(1)

    entry = part_v[...]
    for d in range(1, ntp):
        other = lax.rem(tp + d, ntp)
        pltpu.make_async_remote_copy(
            src_ref=part_v,
            dst_ref=tp_in.at[other],
            send_sem=tp_send.at[d - 1],
            recv_sem=tp_recv.at[other],
            device_id={"tp": other},
            device_id_type=MESH,
        ).wait_recv()
        entry = entry + tp_in[other]

    for t in range(T):
        ebc_v[t * N : (t + 1) * N, :] = jnp.broadcast_to(entry[:N, t : t + 1], (N, 128))
    hi = lax.Precision.HIGHEST
    rows = lax.broadcasted_iota(jnp.int32, (T, T), 0)
    cols = lax.broadcasted_iota(jnp.int32, (T, T), 1)
    by_pos = nt_dot((rows == cols).astype(F32), entry, hi)
    width = CHUNK * N
    srow = lax.broadcasted_iota(jnp.int32, (2 * N, width), 0)
    scol = lax.broadcasted_iota(jnp.int32, (2 * N, width), 1)
    pick = (srow == N + lax.rem(scol, N)).astype(F32)
    spread = jnp.dot(by_pos, pick, precision=hi, preferred_element_type=F32)
    mrow = lax.rem(lax.broadcasted_iota(jnp.int32, (T, width), 0), CHUNK)
    mcol = lax.div(lax.broadcasted_iota(jnp.int32, (T, width), 1), N)
    rb_v[...] = jnp.where(mrow == mcol, spread, 0.0).astype(BF16)

    tiles = W // 128

    def run(group_at, start, driven):
        lanes = pl.ds(pl.multiple_of(group_at * W, W), W)
        rate = -decay_ref[:, lanes]
        rates = [rate[:, c * 128 : (c + 1) * 128] for c in range(tiles)]

        def turn(i, states):
            states = list(states)
            before = None
            for k in range(UNROLL):
                t = i * UNROLL + k
                row = pl.ds(t, N, stride=0)
                if driven:
                    e = ebc_v[pl.ds(pl.multiple_of(t * N, N), N), :]
                for c in range(tiles):
                    at = group_at * tiles + c
                    states[c] = jnp.exp(rates[c] * step_v[at, row, :]) * states[c]
                    if driven:
                        states[c] = states[c] + e * drive_v[at, row, :]
                if k % 2 == 0:
                    before = list(states)
                else:
                    for c in range(tiles):
                        h_v[
                            pl.ds(pl.multiple_of((t - 1) * N, 2 * N), 2 * N),
                            c * 128 : (c + 1) * 128,
                        ] = jnp.concatenate([before[c], states[c]], axis=0).astype(BF16)
            return tuple(states)

        start = tuple(start[:, c * 128 : (c + 1) * 128] for c in range(tiles))
        return jnp.concatenate(lax.fori_loop(0, T // UNROLL, turn, start), axis=1)

    def read_out(k):
        return jnp.dot(
            rb_v[k * CHUNK : (k + 1) * CHUNK, :],
            h_v[k * width : (k + 1) * width, :],
            preferred_element_type=F32,
        )

    half = W // 2

    def chain_copy(g):
        return pltpu.make_async_remote_copy(
            src_ref=chain_out.at[g],
            dst_ref=chain_in.at[g],
            send_sem=chain_send.at[g],
            recv_sem=chain_recv.at[g],
            device_id={"ctx": later},
            device_id_type=MESH,
        )

    def hand_down(g):
        lanes = pl.ds(pl.multiple_of(g * W, W), W)

        @pl.when(me == 0)
        def _():
            ent_v[:, lanes] = jnp.zeros((N, W), F32)

        @pl.when(me > 0)
        def _():
            chain_copy(g).wait_recv()
            both = chain_in[g].astype(F32)
            ent_v[:, lanes] = jnp.concatenate([both[:N], both[N:]], axis=1)

        @pl.when(me + 1 < nctx)
        def _():
            out = dtot_v[:, lanes] * ent_v[:, lanes] + hend_v[:, lanes]
            chain_out[g] = jnp.concatenate([out[:, :half], out[:, half:]], axis=0).astype(BF16)
            chain_copy(g).start()

    local[9].wait()

    def mam_copy(g):
        lanes = pl.ds(pl.multiple_of(g * W, W), W)
        return pltpu.make_async_remote_copy(
            src_ref=mam_stage.at[:, lanes],
            dst_ref=mam_out.at[:, lanes],
            send_sem=mam_send.at[g],
            recv_sem=mam_recv.at[g],
            device_id={"pipe": nxt},
            device_id_type=MESH,
        )

    def leave(g):
        lanes = pl.ds(pl.multiple_of(g * W, W), W)
        for k in range(T // CHUNK):
            part = slice(k * CHUNK, (k + 1) * CHUNK)
            gate = gate_v[part, lanes].astype(F32)
            mam_stage[part, lanes] = (y_v[part, lanes] * silu(gate)).astype(BF16)
        mam_copy(g).start()

    @pl.loop(0, G)
    def _(g):
        lanes = pl.ds(pl.multiple_of(g * W, W), W)
        hend_v[:, lanes] = run(g, jnp.zeros((N, W), F32), True)
        for k in range(T // CHUNK):
            part = slice(k * CHUNK, (k + 1) * CHUNK)
            y_v[part, lanes] = read_out(k) + skip_ref[:, lanes] * act_v[part, lanes].astype(F32)

        @pl.when(g >= me)
        def _():
            hand_down(g - me)

        @pl.when(me == 0)
        def _():
            leave(g)

        @pl.when((g >= 1) & (g + 1 <= me) & (me + 1 < nctx))
        def _():
            kv_pass(g + 1)

    def finish(g):
        lanes = pl.ds(pl.multiple_of(g * W, W), W)
        run(g, ent_v[:, lanes], False)
        for k in range(T // CHUNK):
            part = slice(k * CHUNK, (k + 1) * CHUNK)
            y_v[part, lanes] += read_out(k)
        leave(g)

    lag = max(0, nctx - 1 - G)

    @pl.loop(0, lag + G)
    def _(i):
        @pl.when((G + i >= me) & (i < me))
        def _():
            hand_down(G + i - me)

        @pl.when((i >= lag) & (me > 0))
        def _():
            finish(i - lag)

    over[1].wait_recv()

    @pl.loop(jnp.where(me + 1 < nctx, G + 1, 1), me + 1)
    def _(r):
        kv_pass(r)

    scale = 1.0 / math.sqrt(D)
    rows_of = lax.broadcasted_iota(jnp.int32, (group * T, T), 0)
    seen = lax.broadcasted_iota(jnp.int32, (group * T, T), 1) <= lax.rem(rows_of, T)
    ones = jnp.ones((T, 128), BF16)

    def att_copy(g):
        heads_of = pl.ds(g * group, group)
        return pltpu.make_async_copy(
            att_stage.at[heads_of], att_out.at[heads_of], att_sem.at[g]
        )

    def query(g):
        return q_v[g * group : (g + 1) * group].reshape(group * T, D)

    for g in range(kvh):
        s = jnp.where(seen, nt_dot(query(g), kv_all[me, g]), -1e30)
        score_v[g, me] = s
        top_v[g] = s

    @pl.loop(0, me)
    def _(j):
        for g in range(kvh):
            s = nt_dot(query(g), kv_all[j, g])
            score_v[g, j] = s
            top_v[g] = jnp.maximum(top_v[g], s)

    for g in range(kvh):
        top_v[g] = jnp.broadcast_to(jnp.max(top_v[g], axis=1, keepdims=True), (group * T, T))

    def weigh(g, j):
        p = jnp.exp((score_v[g, j] - top_v[g]) * scale).astype(BF16)
        values = jnp.concatenate([kv_all[j, kvh + g], ones], axis=1)
        return jnp.dot(p, values, preferred_element_type=F32)

    for g in range(kvh):
        acc = lax.fori_loop(0, me, lambda j, acc, g=g: acc + weigh(g, j), weigh(g, me))
        out = (acc[:, :D] / acc[:, D:]).astype(BF16)
        heads_of = slice(g * group, (g + 1) * group)
        att_stage[heads_of] = out.reshape(group, T, D)
        att_copy(g).start()

    @pl.when(me + 1 < nctx)
    def _():
        halo_copy.wait_send()

        @pl.loop(0, G)
        def _(g):
            chain_copy(g).wait_send()

    @pl.when(me + 1 < nctx)
    def _():
        @pl.loop(0, me + 1)
        def _(r):
            kv_copy(r).wait_send()

    for d in range(1, ntp):
        tp_copy(d).wait_send()
    for copy in over:
        copy.wait_send()
    for g in range(kvh):
        att_copy(g).wait()

    @pl.loop(0, G)
    def _(g):
        mam_copy(g).wait()


def per_device(
    sizes,
    queries,
    key_value,
    mamba_in,
    gate_in,
    step_low,
    step_weight,
    step_bias,
    decay_rate,
    conv_weight,
    conv_bias,
    state_weight,
    skip_gain,
):
    nctx, ntp, _ = sizes
    T, H, D = queries.shape[1:]
    kvh = key_value.shape[3]
    C = mamba_in.shape[2]
    R = step_low.shape[2]
    N = decay_rate.shape[1]
    W = min(1024, C // 2)
    B = 256
    q = jnp.transpose(queries[0], (1, 0, 2))
    kv = jnp.transpose(key_value[0], (0, 2, 1, 3)).reshape(2 * kvh, T, D)
    anywhere = pl.BlockSpec(memory_space=pl.ANY)
    dma = pltpu.SemaphoreType.DMA
    att, mam = pl.pallas_call(
        functools.partial(kernel, sizes),
        out_shape=(
            jax.ShapeDtypeStruct((H, T, D), BF16),
            jax.ShapeDtypeStruct((T, C), BF16),
        ),
        in_specs=[anywhere] * 12,
        out_specs=(anywhere, anywhere),
        scratch_shapes=[
            pltpu.VMEM((H, T, D), BF16),
            pltpu.VMEM((kvh, nctx, H // kvh * T, T), F32),
            pltpu.VMEM((kvh, H // kvh * T, T), F32),
            pltpu.VMEM((T, C), BF16),
            pltpu.VMEM((T, C), BF16),
            pltpu.VMEM((T, R), BF16),
            pltpu.VMEM((R, C), BF16),
            pltpu.VMEM((1, C), F32),
            pltpu.VMEM((N, C), F32),
            pltpu.VMEM(conv_weight.shape[1:], F32),
            pltpu.VMEM((1, C), F32),
            pltpu.VMEM((2 * N, C), BF16),
            pltpu.VMEM((1, C), F32),
            pltpu.VMEM((nctx, 2 * kvh, T, D), BF16),
            pltpu.VMEM((HALO, C), BF16),
            pltpu.VMEM((HALO + T, B), F32),
            pltpu.VMEM((T, C), BF16),
            pltpu.VMEM((C // 128, T, 128), F32),
            pltpu.VMEM((C // 128, T, 128), F32),
            pltpu.VMEM((T, C), F32),
            pltpu.VMEM((T * N, W), BF16),
            pltpu.VMEM((T * N, 128), F32),
            pltpu.VMEM((T, CHUNK * N), BF16),
            pltpu.VMEM((2 * N, T), F32),
            pltpu.VMEM((ntp, 2 * N, T), F32),
            pltpu.VMEM((N, C), F32),
            pltpu.VMEM((N, C), F32),
            pltpu.VMEM((N, C), F32),
            pltpu.VMEM((C // W, 2 * N, W // 2), BF16),
            pltpu.VMEM((C // W, 2 * N, W // 2), BF16),
            pltpu.VMEM((H, T, D), BF16),
            pltpu.VMEM((T, C), BF16),
            dma((10,)),
            dma((2,)),
            dma((nctx,)),
            dma((nctx,)),
            dma((max(1, ntp - 1),)),
            dma((ntp,)),
            dma((C // W,)),
            dma((C // W,)),
            dma((kvh,)),
            dma((2,)),
            dma((2,)),
            dma((C // W,)),
            dma((C // W,)),
        ],
        compiler_params=pltpu.CompilerParams(
            collective_id=0, has_side_effects=True, vmem_limit_bytes=60 * 2**20
        ),
    )(
        q,
        kv,
        mamba_in[0],
        gate_in[0],
        step_low[0],
        step_weight[0],
        step_bias,
        decay_rate[0],
        conv_weight[0],
        conv_bias,
        state_weight[0].T,
        skip_gain,
    )
    return jnp.transpose(att, (1, 0, 2))[None], mam[None]


def solution(mesh):
    sizes = (mesh.shape["ctx"], mesh.shape["tp"], mesh.shape["pipe"])
    return jax.shard_map(
        functools.partial(per_device, sizes),
        mesh=mesh,
        in_specs=(
            P("pipe", "ctx", "tp", None),
            P("pipe", None, "ctx", "tp", None),
            P("pipe", "ctx", "tp"),
            P("pipe", "ctx", "tp"),
            P("pipe", "ctx", None),
            P("pipe", None, "tp"),
            P("pipe", "tp"),
            P("pipe", None, "tp"),
            P("pipe", None, "tp"),
            P("pipe", "tp"),
            P("pipe", "tp", None),
            P("pipe", "tp"),
        ),
        out_specs=(P("pipe", "ctx", "tp", None), P("pipe", "ctx", "tp")),
        check_vma=False,
    )
```

```python
import functools
import math

import jax
import jax.numpy as jnp
from jax import lax
from jax.experimental import pallas as pl
from jax.experimental.pallas import tpu as pltpu
from jax.sharding import PartitionSpec as P

F32 = jnp.float32
BF16 = jnp.bfloat16
MESH = pl.DeviceIdType.MESH
CHUNK = 32
HALO = 16
UNROLL = 16


def nt_dot(a, b, precision=None):
    return lax.dot_general(
        a, b, (((1,), (1,)), ((), ())), precision=precision, preferred_element_type=F32
    )


def silu(v):
    return 0.5 * v * (1.0 + jnp.tanh(0.5 * v))


def kernel(
    sizes,
    q_hbm,
    kv_hbm,
    x_hbm,
    gate_hbm,
    low_hbm,
    sw_hbm,
    bias_hbm,
    decay_hbm,
    cw_hbm,
    cb_hbm,
    ew_hbm,
    skip_hbm,
    att_out,
    mam_out,
    q_v,
    score_v,
    top_v,
    x_v,
    gate_v,
    low_v,
    sw_v,
    bias_ref,
    decay_ref,
    cw_ref,
    cb_ref,
    ew_ref,
    skip_ref,
    kv_all,
    halo,
    pad_v,
    act_v,
    step_v,
    drive_v,
    y_v,
    h_v,
    ebc_v,
    rb_v,
    part_v,
    tp_in,
    hend_v,
    ent_v,
    dtot_v,
    chain_out,
    chain_in,
    att_stage,
    mam_stage,
    local_sem,
    halo_sem,
    kv_send,
    kv_recv,
    tp_send,
    tp_recv,
    chain_send,
    chain_recv,
    att_sem,
    over_send,
    over_recv,
    mam_send,
    mam_recv,
):
    nctx, ntp, npipe = sizes
    T, C = x_v.shape
    heads, _, D = q_v.shape
    kvh = kv_all.shape[1] // 2
    group = heads // kvh
    N = decay_ref.shape[0]
    taps = cw_ref.shape[0]
    W = h_v.shape[1]
    G = C // W
    B = pad_v.shape[1]

    me = lax.axis_index("ctx")
    tp = lax.axis_index("tp")
    pipe = lax.axis_index("pipe")
    nxt = lax.rem(pipe + 1, npipe)
    prv = lax.rem(pipe + npipe - 1, npipe)

    local = []
    for i, (src, dst) in enumerate(
        (
            (x_hbm, x_v),
            (cw_hbm, cw_ref),
            (cb_hbm, cb_ref),
            (ew_hbm, ew_ref),
            (low_hbm, low_v),
            (sw_hbm, sw_v),
            (bias_hbm, bias_ref),
            (decay_hbm, decay_ref),
            (skip_hbm, skip_ref),
            (gate_hbm, gate_v),
        )
    ):
        copy = pltpu.make_async_copy(src, dst, local_sem.at[i])
        copy.start()
        local.append(copy)

    barrier = pltpu.get_barrier_semaphore()
    for d in range(1, nctx):
        pl.semaphore_signal(
            barrier, inc=1, device_id={"ctx": lax.rem(me + d, nctx)}, device_id_type=MESH
        )
    for d in range(1, ntp):
        pl.semaphore_signal(
            barrier, inc=1, device_id={"tp": lax.rem(tp + d, ntp)}, device_id_type=MESH
        )
    pl.semaphore_signal(barrier, inc=1, device_id={"pipe": nxt}, device_id_type=MESH)
    pl.semaphore_signal(barrier, inc=1, device_id={"pipe": prv}, device_id_type=MESH)
    pl.semaphore_wait(barrier, nctx - 1 + ntp - 1 + 2)

    later = jnp.minimum(me + 1, nctx - 1)
    halo_copy = pltpu.make_async_remote_copy(
        src_ref=x_hbm.at[pl.ds(T - HALO, HALO)],
        dst_ref=halo,
        send_sem=halo_sem.at[0],
        recv_sem=halo_sem.at[1],
        device_id={"ctx": later},
        device_id_type=MESH,
    )

    @pl.when(me + 1 < nctx)
    def _():
        halo_copy.start()

    over = []
    for i, (src, dst) in enumerate(((kv_hbm, kv_all.at[me]), (q_hbm, q_v))):
        copy = pltpu.make_async_remote_copy(
            src_ref=src,
            dst_ref=dst,
            send_sem=over_send.at[i],
            recv_sem=over_recv.at[i],
            device_id={"pipe": nxt},
            device_id_type=MESH,
        )
        copy.start()
        over.append(copy)

    def kv_copy(r):
        j = jnp.maximum(me - r, 0)
        return pltpu.make_async_remote_copy(
            src_ref=kv_all.at[j],
            dst_ref=kv_all.at[j],
            send_sem=kv_send.at[r],
            recv_sem=kv_recv.at[j],
            device_id={"ctx": later},
            device_id_type=MESH,
        )

    def kv_pass(r):
        kv_copy(r).wait_recv()

        @pl.when(me + 1 < nctx)
        def _():
            kv_copy(r).start()

    for copy in local[:4]:
        copy.wait()

    @pl.when(me > 0)
    def _():
        halo_copy.wait_recv()

    @pl.when(me == 0)
    def _():
        halo[...] = jnp.zeros_like(halo)

    over[0].wait_recv()

    @pl.when(me + 1 < nctx)
    def _():
        kv_copy(0).start()

    part_v[...] = jnp.zeros_like(part_v)

    @pl.loop(0, C // B)
    def _(b):
        lanes = pl.ds(pl.multiple_of(b * B, B), B)
        pad_v[0:HALO, :] = halo[:, lanes].astype(F32)
        pad_v[HALO:, :] = x_v[:, lanes].astype(F32)
        conv = cb_ref[:, lanes]
        for k in range(taps):
            conv = conv + cw_ref[k : k + 1, lanes] * pad_v[pl.ds(HALO - (taps - 1) + k, T), :]
        act = silu(conv).astype(BF16)
        act_v[:, lanes] = act
        part_v[...] += nt_dot(ew_ref[:, lanes], act)

    def tp_copy(d):
        return pltpu.make_async_remote_copy(
            src_ref=part_v,
            dst_ref=tp_in.at[tp],
            send_sem=tp_send.at[d - 1],
            recv_sem=tp_recv.at[tp],
            device_id={"tp": lax.rem(tp + d, ntp)},
            device_id_type=MESH,
        )

    for d in range(1, ntp):
        tp_copy(d).start()

    for copy in local[4:9]:
        copy.wait()

    @pl.loop(0, C // B)
    def _(b):
        lanes = pl.ds(pl.multiple_of(b * B, B), B)
        v = jnp.dot(low_v[...], sw_v[:, lanes], preferred_element_type=F32) + bias_ref[:, lanes]
        step = jnp.maximum(v, 0.0) + jnp.log1p(jnp.exp(-jnp.abs(v)))
        drive = step * act_v[:, lanes].astype(F32)
        for i in range(B // 128):
            cols = slice(i * 128, (i + 1) * 128)
            step_v[b * (B // 128) + i] = step[:, cols]
            drive_v[b * (B // 128) + i] = drive[:, cols]
        dtot_v[:, lanes] = jnp.exp(
            -decay_ref[:, lanes] * jnp.sum(step, axis=0, keepdims=True)
        )

    @pl.when((me >= 1) & (me + 1 < nctx))
    def _():
        kv_pass(1)

    entry = part_v[...]
    for d in range(1, ntp):
        other = lax.rem(tp + d, ntp)
        pltpu.make_async_remote_copy(
            src_ref=part_v,
            dst_ref=tp_in.at[other],
            send_sem=tp_send.at[d - 1],
            recv_sem=tp_recv.at[other],
            device_id={"tp": other},
            device_id_type=MESH,
        ).wait_recv()
        entry = entry + tp_in[other]

    for t in range(T):
        ebc_v[t * N : (t + 1) * N, :] = jnp.broadcast_to(entry[:N, t : t + 1], (N, 128))
    hi = lax.Precision.HIGHEST
    rows = lax.broadcasted_iota(jnp.int32, (T, T), 0)
    cols = lax.broadcasted_iota(jnp.int32, (T, T), 1)
    by_pos = nt_dot((rows == cols).astype(F32), entry, hi)
    width = CHUNK * N
    srow = lax.broadcasted_iota(jnp.int32, (2 * N, width), 0)
    scol = lax.broadcasted_iota(jnp.int32, (2 * N, width), 1)
    pick = (srow == N + lax.rem(scol, N)).astype(F32)
    spread = jnp.dot(by_pos, pick, precision=hi, preferred_element_type=F32)
    mrow = lax.rem(lax.broadcasted_iota(jnp.int32, (T, width), 0), CHUNK)
    mcol = lax.div(lax.broadcasted_iota(jnp.int32, (T, width), 1), N)
    rb_v[...] = jnp.where(mrow == mcol, spread, 0.0).astype(BF16)

    tiles = W // 128

    def run(group_at, start, driven):
        lanes = pl.ds(pl.multiple_of(group_at * W, W), W)
        rate = -decay_ref[:, lanes]
        rates = [rate[:, c * 128 : (c + 1) * 128] for c in range(tiles)]

        def turn(i, states):
            states = list(states)
            before = None
            for k in range(UNROLL):
                t = i * UNROLL + k
                row = pl.ds(t, N, stride=0)
                if driven:
                    e = ebc_v[pl.ds(pl.multiple_of(t * N, N), N), :]
                for c in range(tiles):
                    at = group_at * tiles + c
                    states[c] = jnp.exp(rates[c] * step_v[at, row, :]) * states[c]
                    if driven:
                        states[c] = states[c] + e * drive_v[at, row, :]
                if k % 2 == 0:
                    before = list(states)
                else:
                    for c in range(tiles):
                        h_v[
                            pl.ds(pl.multiple_of((t - 1) * N, 2 * N), 2 * N),
                            c * 128 : (c + 1) * 128,
                        ] = jnp.concatenate([before[c], states[c]], axis=0).astype(BF16)
            return tuple(states)

        start = tuple(start[:, c * 128 : (c + 1) * 128] for c in range(tiles))
        return jnp.concatenate(lax.fori_loop(0, T // UNROLL, turn, start), axis=1)

    def read_out(k):
        return jnp.dot(
            rb_v[k * CHUNK : (k + 1) * CHUNK, :],
            h_v[k * width : (k + 1) * width, :],
            preferred_element_type=F32,
        )

    half = W // 2

    def chain_copy(g):
        return pltpu.make_async_remote_copy(
            src_ref=chain_out.at[g],
            dst_ref=chain_in.at[g],
            send_sem=chain_send.at[g],
            recv_sem=chain_recv.at[g],
            device_id={"ctx": later},
            device_id_type=MESH,
        )

    def hand_down(g):
        lanes = pl.ds(pl.multiple_of(g * W, W), W)

        @pl.when(me == 0)
        def _():
            ent_v[:, lanes] = jnp.zeros((N, W), F32)

        @pl.when(me > 0)
        def _():
            chain_copy(g).wait_recv()
            both = chain_in[g].astype(F32)
            ent_v[:, lanes] = jnp.concatenate([both[:N], both[N:]], axis=1)

        @pl.when(me + 1 < nctx)
        def _():
            out = dtot_v[:, lanes] * ent_v[:, lanes] + hend_v[:, lanes]
            chain_out[g] = jnp.concatenate([out[:, :half], out[:, half:]], axis=0).astype(BF16)
            chain_copy(g).start()

    local[9].wait()

    def mam_copy(g):
        lanes = pl.ds(pl.multiple_of(g * W, W), W)
        return pltpu.make_async_remote_copy(
            src_ref=mam_stage.at[:, lanes],
            dst_ref=mam_out.at[:, lanes],
            send_sem=mam_send.at[g],
            recv_sem=mam_recv.at[g],
            device_id={"pipe": nxt},
            device_id_type=MESH,
        )

    def leave(g):
        lanes = pl.ds(pl.multiple_of(g * W, W), W)
        for k in range(T // CHUNK):
            part = slice(k * CHUNK, (k + 1) * CHUNK)
            gate = gate_v[part, lanes].astype(F32)
            mam_stage[part, lanes] = (y_v[part, lanes] * silu(gate)).astype(BF16)
        mam_copy(g).start()

    @pl.loop(0, G)
    def _(g):
        lanes = pl.ds(pl.multiple_of(g * W, W), W)
        hend_v[:, lanes] = run(g, jnp.zeros((N, W), F32), True)
        for k in range(T // CHUNK):
            part = slice(k * CHUNK, (k + 1) * CHUNK)
            y_v[part, lanes] = read_out(k) + skip_ref[:, lanes] * act_v[part, lanes].astype(F32)

        @pl.when(g >= me)
        def _():
            hand_down(g - me)

        @pl.when(me == 0)
        def _():
            leave(g)

        @pl.when((g >= 1) & (g + 1 <= me) & (me + 1 < nctx))
        def _():
            kv_pass(g + 1)

    def finish(g):
        lanes = pl.ds(pl.multiple_of(g * W, W), W)
        run(g, ent_v[:, lanes], False)
        for k in range(T // CHUNK):
            part = slice(k * CHUNK, (k + 1) * CHUNK)
            y_v[part, lanes] += read_out(k)
        leave(g)

    lag = max(0, nctx - 1 - G)

    @pl.loop(0, lag + G)
    def _(i):
        @pl.when((G + i >= me) & (i < me))
        def _():
            hand_down(G + i - me)

        @pl.when((i >= lag) & (me > 0))
        def _():
            finish(i - lag)

    over[1].wait_recv()

    @pl.loop(jnp.where(me + 1 < nctx, G + 1, 1), me + 1)
    def _(r):
        kv_pass(r)

    scale = 1.0 / math.sqrt(D)
    rows_of = lax.broadcasted_iota(jnp.int32, (group * T, T), 0)
    seen = lax.broadcasted_iota(jnp.int32, (group * T, T), 1) <= lax.rem(rows_of, T)
    ones = jnp.ones((T, 128), BF16)

    def att_copy(g):
        heads_of = pl.ds(g * group, group)
        return pltpu.make_async_copy(
            att_stage.at[heads_of], att_out.at[heads_of], att_sem.at[g]
        )

    def query(g):
        return q_v[g * group : (g + 1) * group].reshape(group * T, D)

    for g in range(kvh):
        s = jnp.where(seen, nt_dot(query(g), kv_all[me, g]), -1e30)
        score_v[g, me] = s
        top_v[g] = s

    @pl.loop(0, me)
    def _(j):
        for g in range(kvh):
            s = nt_dot(query(g), kv_all[j, g])
            score_v[g, j] = s
            top_v[g] = jnp.maximum(top_v[g], s)

    for g in range(kvh):
        top_v[g] = jnp.broadcast_to(jnp.max(top_v[g], axis=1, keepdims=True), (group * T, T))

    def weigh(g, j):
        p = jnp.exp((score_v[g, j] - top_v[g]) * scale).astype(BF16)
        values = jnp.concatenate([kv_all[j, kvh + g], ones], axis=1)
        return jnp.dot(p, values, preferred_element_type=F32)

    for g in range(kvh):
        acc = lax.fori_loop(0, me, lambda j, acc, g=g: acc + weigh(g, j), weigh(g, me))
        out = (acc[:, :D] / acc[:, D:]).astype(BF16)
        heads_of = slice(g * group, (g + 1) * group)
        att_stage[heads_of] = out.reshape(group, T, D)
        att_copy(g).start()

    @pl.when(me + 1 < nctx)
    def _():
        halo_copy.wait_send()

        @pl.loop(0, G)
        def _(g):
            chain_copy(g).wait_send()

    @pl.when(me + 1 < nctx)
    def _():
        @pl.loop(0, me + 1)
        def _(r):
            kv_copy(r).wait_send()

    for d in range(1, ntp):
        tp_copy(d).wait_send()
    for copy in over:
        copy.wait_send()
    for g in range(kvh):
        att_copy(g).wait()

    @pl.loop(0, G)
    def _(g):
        mam_copy(g).wait()


def per_device(
    sizes,
    queries,
    key_value,
    mamba_in,
    gate_in,
    step_low,
    step_weight,
    step_bias,
    decay_rate,
    conv_weight,
    conv_bias,
    state_weight,
    skip_gain,
):
    nctx, ntp, _ = sizes
    T, H, D = queries.shape[1:]
    kvh = key_value.shape[3]
    C = mamba_in.shape[2]
    R = step_low.shape[2]
    N = decay_rate.shape[1]
    W = min(1024, C // 2)
    B = min(512, C // 2)
    q = jnp.transpose(queries[0], (1, 0, 2))
    kv = jnp.transpose(key_value[0], (0, 2, 1, 3)).reshape(2 * kvh, T, D)
    anywhere = pl.BlockSpec(memory_space=pl.ANY)
    dma = pltpu.SemaphoreType.DMA
    att, mam = pl.pallas_call(
        functools.partial(kernel, sizes),
        out_shape=(
            jax.ShapeDtypeStruct((H, T, D), BF16),
            jax.ShapeDtypeStruct((T, C), BF16),
        ),
        in_specs=[anywhere] * 12,
        out_specs=(anywhere, anywhere),
        scratch_shapes=[
            pltpu.VMEM((H, T, D), BF16),
            pltpu.VMEM((kvh, nctx, H // kvh * T, T), F32),
            pltpu.VMEM((kvh, H // kvh * T, T), F32),
            pltpu.VMEM((T, C), BF16),
            pltpu.VMEM((T, C), BF16),
            pltpu.VMEM((T, R), BF16),
            pltpu.VMEM((R, C), BF16),
            pltpu.VMEM((1, C), F32),
            pltpu.VMEM((N, C), F32),
            pltpu.VMEM(conv_weight.shape[1:], F32),
            pltpu.VMEM((1, C), F32),
            pltpu.VMEM((2 * N, C), BF16),
            pltpu.VMEM((1, C), F32),
            pltpu.VMEM((nctx, 2 * kvh, T, D), BF16),
            pltpu.VMEM((HALO, C), BF16),
            pltpu.VMEM((HALO + T, B), F32),
            pltpu.VMEM((T, C), BF16),
            pltpu.VMEM((C // 128, T, 128), F32),
            pltpu.VMEM((C // 128, T, 128), F32),
            pltpu.VMEM((T, C), F32),
            pltpu.VMEM((T * N, W), BF16),
            pltpu.VMEM((T * N, 128), F32),
            pltpu.VMEM((T, CHUNK * N), BF16),
            pltpu.VMEM((2 * N, T), F32),
            pltpu.VMEM((ntp, 2 * N, T), F32),
            pltpu.VMEM((N, C), F32),
            pltpu.VMEM((N, C), F32),
            pltpu.VMEM((N, C), F32),
            pltpu.VMEM((C // W, 2 * N, W // 2), BF16),
            pltpu.VMEM((C // W, 2 * N, W // 2), BF16),
            pltpu.VMEM((H, T, D), BF16),
            pltpu.VMEM((T, C), BF16),
            dma((10,)),
            dma((2,)),
            dma((nctx,)),
            dma((nctx,)),
            dma((max(1, ntp - 1),)),
            dma((ntp,)),
            dma((C // W,)),
            dma((C // W,)),
            dma((kvh,)),
            dma((2,)),
            dma((2,)),
            dma((C // W,)),
            dma((C // W,)),
        ],
        compiler_params=pltpu.CompilerParams(
            collective_id=0, has_side_effects=True, vmem_limit_bytes=60 * 2**20
        ),
    )(
        q,
        kv,
        mamba_in[0],
        gate_in[0],
        step_low[0],
        step_weight[0],
        step_bias,
        decay_rate[0],
        conv_weight[0],
        conv_bias,
        state_weight[0].T,
        skip_gain,
    )
    return jnp.transpose(att, (1, 0, 2))[None], mam[None]


def solution(mesh):
    sizes = (mesh.shape["ctx"], mesh.shape["tp"], mesh.shape["pipe"])
    return jax.shard_map(
        functools.partial(per_device, sizes),
        mesh=mesh,
        in_specs=(
            P("pipe", "ctx", "tp", None),
            P("pipe", None, "ctx", "tp", None),
            P("pipe", "ctx", "tp"),
            P("pipe", "ctx", "tp"),
            P("pipe", "ctx", None),
            P("pipe", None, "tp"),
            P("pipe", "tp"),
            P("pipe", None, "tp"),
            P("pipe", None, "tp"),
            P("pipe", "tp"),
            P("pipe", "tp", None),
            P("pipe", "tp"),
        ),
        out_specs=(P("pipe", "ctx", "tp", None), P("pipe", "ctx", "tp")),
        check_vma=False,
    )
```
